256 devices in a mesh: feed: 32 (over z, x), tm: 8 (over y, core).
Axes of the slice: x: 4, y: 4, z: 8, core: 2. Of those that a mesh axis runs over, the one named last changes fastest.
Arguments:
- voltages: bfloat16 [2048, 262144], P('feed', 'tm'), may hold values from -6 to 6
- feed_slot: int32 [2048], replicated, may hold values from 0 to 2047, each once
- channel_flags: int32 [1024], replicated, may hold values from 0 to 1, as said below
Outputs:
- beam_power: float32 [768, 16, 1024], P(('feed', 'tm'))
The draws below stay inside these ranges and needn't reach their ends.
Inputs may be any that keep to these rules, and one draw needn't show every extreme that they name: `channel_flags`: exactly 768 entries are 1. `feed_slot`: each slot is named by exactly one input.
All inputs are finite; a program needn't handle non-finite values.
Results may differ from the reference program's by a relative error of at most 0.01.
Values may be sent and summed in bfloat16 or wider, within the bound.
No kernel may reach another device: no remote copies, remote signals or barrier semaphores. Data moves between devices by JAX's collectives and lax.ppermute only.
A program may use at most 128 MiB of HBM per device.

```python
import math
import jax
import jax.numpy as jnp
from jax import lax

CHANNELS = 1024
TAPS = 4
CYL = 4
NS = 256
UPCH = 16
FRAME = 2048
INPUTS = 2048
FR_DEV = 16
IN_DEV = 64
LIVE = 768
N_TM = 8


def draw_channel_flags(key, part):
    shuffled = jax.random.permutation(jax.random.fold_in(key, 11), CHANNELS)
    return (shuffled < LIVE).astype(jnp.int32)


def shard_levels(rng, shape, split, least, top_value):
    def one(position, parts):
        heights = jax.random.uniform(jax.random.fold_in(jax.random.fold_in(rng, 6), position), (parts,), jnp.float32, least / len(split), top_value / len(split))
        return jnp.repeat(jnp.exp(heights), shape[position] // parts).reshape((-1,) + (1,) * (len(shape) - position - 1))

    level = one(*split[0])
    for cut in split[1:]:
        level = level * one(*cut)
    return level


def normal_values(own_key, extent, width, reach, shards=(), kind=jnp.bfloat16):
    gain = shard_levels(own_key, extent, shards, -0.22, 0.18) if shards else 1.0
    entries = jax.random.normal(own_key, extent, jnp.float32) * width * gain
    return jnp.minimum(jnp.maximum(entries, -reach), reach).astype(kind)


def setup_inputs(seed: int = 0) -> dict:
    keys = jax.random.split(jax.random.key(seed), 4)
    return {
        "voltages": normal_values(keys[0], (INPUTS, N_TM * FR_DEV * FRAME), 1.0, 6.0, ((0, 32), (1, 8))),
        "feed_slot": jax.random.permutation(keys[1], INPUTS).astype(jnp.int32),
        "channel_flags": draw_channel_flags(jax.random.fold_in(keys[3], 71), 0),
    }


def pfb_window():
    length = TAPS * 2 * CHANNELS
    sample = jnp.arange(length, dtype=jnp.float32)
    offset = (sample - length / 2 + 0.5) / (2 * CHANNELS)
    taper = 0.5 - 0.5 * jnp.cos(2.0 * jnp.pi * (sample + 0.5) / length)
    return (jnp.sinc(offset) * taper).reshape(TAPS, 2 * CHANNELS)

def phase_pair(modulus, first, second, scale):
    product = jnp.arange(first, dtype=jnp.int32)[:, None] * jnp.arange(second, dtype=jnp.int32)[None, :] % modulus
    angle = product.astype(jnp.float32) * (2.0 * jnp.pi / modulus)
    return (jnp.cos(angle) * scale, jnp.sin(angle) * scale)

def channel_table():
    cosine, sine = phase_pair(2 * CHANNELS, CHANNELS, 2 * CHANNELS, 1.0 / math.sqrt(2 * CHANNELS))
    return jnp.stack([cosine, -sine]).astype(jnp.bfloat16)

def grid_table():
    cosine, sine = phase_pair(NS, NS, NS, 1.0 / math.sqrt(NS))
    cosine = cosine.astype(jnp.bfloat16)
    sine = sine.astype(jnp.bfloat16)
    return jnp.stack([jnp.stack([cosine, -sine], axis=1), jnp.stack([sine, cosine], axis=1)])

def pfb_filter(extended, n_frames):
    window = pfb_window()
    summed = jnp.zeros((extended.shape[0], n_frames, extended.shape[2]), jnp.float32)
    for tap_index in range(TAPS):
        summed = summed + window[tap_index] * extended[:, tap_index:tap_index + n_frames].astype(jnp.float32)
    return summed.astype(jnp.bfloat16)

def beamform(spectra, inverse):
    highest = lax.Precision.HIGHEST
    chans, frames = (spectra.shape[0], spectra.shape[1])
    cells = jnp.take(spectra, inverse, axis=3).reshape(chans, frames, 2, 2, CYL, NS)
    ns_out = jnp.einsum('cfrpym,rmqn->cfpyqn', cells.astype(jnp.float32), grid_table().astype(jnp.float32), precision=highest)
    real_part = ns_out[:, :, :, :, 0]
    imag_part = ns_out[:, :, :, :, 1]
    ew_cos, ew_sin = phase_pair(CYL, CYL, CYL, 1.0 / math.sqrt(CYL))
    beam_re = jnp.einsum('cfpyn,ye->cfpen', real_part, ew_cos, precision=highest) + jnp.einsum('cfpyn,ye->cfpen', imag_part, ew_sin, precision=highest)
    beam_im = jnp.einsum('cfpyn,ye->cfpen', imag_part, ew_cos, precision=highest) - jnp.einsum('cfpyn,ye->cfpen', real_part, ew_sin, precision=highest)
    return jnp.stack([beam_re, beam_im], axis=2).astype(jnp.bfloat16)

def block_power(beams, blocks):
    highest = lax.Precision.HIGHEST
    chans = beams.shape[0]
    shaped = beams.reshape(chans, blocks, UPCH, 2, 2, CYL, NS).astype(jnp.float32)
    beam_re = shaped[:, :, :, 0]
    beam_im = shaped[:, :, :, 1]
    up_cos, up_sin = phase_pair(UPCH, UPCH, UPCH, 1.0 / math.sqrt(UPCH))
    up_cos = up_cos.astype(jnp.bfloat16).astype(jnp.float32)
    up_sin = up_sin.astype(jnp.bfloat16).astype(jnp.float32)
    up_re = jnp.einsum('cbupen,uk->cbkpen', beam_re, up_cos, precision=highest) + jnp.einsum('cbupen,uk->cbkpen', beam_im, up_sin, precision=highest)
    up_im = jnp.einsum('cbupen,uk->cbkpen', beam_im, up_cos, precision=highest) - jnp.einsum('cbupen,uk->cbkpen', beam_re, up_sin, precision=highest)
    summed = lax.optimization_barrier(jnp.sum(up_re * up_re + up_im * up_im, axis=(1, 3)))
    return summed.reshape(chans, UPCH, CYL * NS)

def reference(voltages, feed_slot, channel_flags):
    frame_len = 2 * CHANNELS
    n_frames = voltages.shape[1] // frame_len
    live_idx = jnp.nonzero(channel_flags, size=LIVE)[0].astype(jnp.int32)
    coeffs = jnp.take(channel_table(), live_idx, axis=1).astype(jnp.float32)

    def spectra_of(row_block):
        padding = jnp.zeros((row_block.shape[0], (TAPS - 1) * frame_len), jnp.bfloat16)
        extended = jnp.concatenate([padding, row_block], axis=1).reshape(row_block.shape[0], n_frames + TAPS - 1, frame_len)
        filtered = pfb_filter(extended, n_frames)
        return jnp.einsum('rcs,ifs->cfri', coeffs, filtered.astype(jnp.float32), precision=lax.Precision.HIGHEST).astype(jnp.bfloat16)
    grouped = voltages.reshape(INPUTS // IN_DEV, IN_DEV, voltages.shape[1])
    spectra = lax.map(spectra_of, grouped)
    spectra = jnp.moveaxis(spectra, 0, 3).reshape(LIVE, n_frames, 2, INPUTS)
    inverse = jnp.argsort(feed_slot).astype(jnp.int32)

    def channel_power(one_channel):
        beams = beamform(one_channel[None], inverse)
        return block_power(beams, n_frames // UPCH)[0]
    power_sum = lax.map(channel_power, spectra)
    return power_sum / (2.0 * (n_frames // UPCH))
```

```python
import math

import jax
import jax.numpy as jnp
import numpy as np
from jax import lax
from jax.experimental import pallas as pl
from jax.experimental.pallas import tpu as pltpu
from jax.sharding import PartitionSpec as P

CHANNELS = 1024
TAPS = 4
CYL = 4
NS = 256
UPCH = 16
FRAME = 2048
N_FEED = 32
N_TM = 8
IN_DEV = 64
FR_DEV = 16
LIVE_DEV = 3
LIVE = 768
EARLY = 4
MIB = 1 << 20


def window_table():
    length = TAPS * FRAME
    sample = np.arange(length, dtype=np.float64)
    offset = (sample - length / 2 + 0.5) / FRAME
    taper = 0.5 - 0.5 * np.cos(2.0 * np.pi * (sample + 0.5) / length)
    return (np.sinc(offset) * taper).reshape(TAPS, FRAME).astype(np.float32)


def cos_sin(modulus, first, second):
    product = np.arange(first)[:, None] * np.arange(second)[None, :] % modulus
    angle = product * (2.0 * np.pi / modulus)
    scale = 1.0 / math.sqrt(modulus)
    return np.cos(angle) * scale, np.sin(angle) * scale


def position_table():
    cosine, sine = cos_sin(NS, NS, NS)
    return np.concatenate([cosine, sine], axis=1)


def sub_channel_table():
    cosine, sine = cos_sin(UPCH, UPCH, UPCH)
    same = np.eye(N_TM)
    real = np.stack([cosine, sine])
    imag = np.stack([-sine, cosine])
    both = np.stack([real, imag])
    return np.einsum("qruk,ts->qtkurs", both, same).reshape(256, 256)


def unit_circle(phase):
    quadrant = (phase + 256) >> 9
    x = (phase - (quadrant << 9)).astype(jnp.float32) * np.float32(2.0 * np.pi / FRAME)
    x2 = x * x
    c = 1.0 + x2 * (-0.5 + x2 * (1.0 / 24 + x2 * (-1.0 / 720 + x2 * (1.0 / 40320))))
    s = x * (1.0 + x2 * (-1.0 / 6 + x2 * (1.0 / 120 + x2 * (-1.0 / 5040 + x2 * (1.0 / 362880)))))
    odd = (quadrant & 1) == 1
    cos_mag = jnp.where(odd, s, c)
    sin_mag = jnp.where(odd, c, s)
    cosine = jnp.where(((quadrant + 1) & 2) == 2, -cos_mag, cos_mag)
    sine = jnp.where((quadrant & 2) == 2, -sin_mag, sin_mag)
    return cosine, sine


def filter_block(window_ref, load, store, frames, lane):
    taps = [window_ref[pl.ds(t, 1), pl.ds(lane, 128)] for t in range(TAPS)]
    for rows in range(0, IN_DEV, 16):
        held = {}
        for f in frames:
            total = None
            for t in range(TAPS):
                g = f - TAPS + 1 + t
                if g not in held:
                    held[g] = load(g, rows).astype(jnp.float32)
                term = taps[t] * held[g]
                total = term if total is None else total + term
            store(f, rows, total.astype(jnp.bfloat16))


def first_kernel(flags_ref, volt_ref, window_ref, table_ref, late_ref, cos_ref, sin_ref, dcos_ref, dsin_ref):
    rows = lax.broadcasted_iota(jnp.int32, (CHANNELS, CHANNELS), 0)
    cols = lax.broadcasted_iota(jnp.int32, (CHANNELS, CHANNELS), 1)
    upto = (rows <= cols).astype(jnp.float32).astype(jnp.bfloat16)
    flags = jnp.broadcast_to(flags_ref[...].astype(jnp.float32), (16, CHANNELS)).astype(jnp.bfloat16)
    count = jnp.dot(flags, upto, preferred_element_type=jnp.float32)[0:1].astype(jnp.int32)
    ones = jnp.ones((CHANNELS, 128), jnp.bfloat16)

    def place(step, carry):
        row = lax.broadcasted_iota(jnp.int32, (64, CHANNELS), 0) + step * 64
        chunk, owner, t = row >> 8, (row >> 3) & 31, row & 7
        rank = owner * (LIVE_DEV * N_TM) + t * LIVE_DEV + chunk
        below = (count <= rank).astype(jnp.float32).astype(jnp.bfloat16)
        channel = jnp.dot(below, ones, preferred_element_type=jnp.float32).astype(jnp.int32)
        at = pl.ds(pl.multiple_of(step * 64, 64), 64)
        lane = lax.broadcasted_iota(jnp.int32, (64, 128), 1)
        c, s = unit_circle((channel * lane) & (FRAME - 1))
        scale = np.float32(1.0 / math.sqrt(FRAME))
        cos_ref[at, :] = c * scale
        sin_ref[at, :] = s * scale
        c, s = unit_circle((channel * 128) & (FRAME - 1))
        dcos_ref[at, :] = c
        dsin_ref[at, :] = s
        return carry

    lax.fori_loop(0, LIVE // 64, place, 0)

    def turn(step, carry):
        at = pl.ds(pl.multiple_of(step * 64, 64), 64)
        c, s = cos_ref[at, :].reshape(8, 8, 128), sin_ref[at, :].reshape(8, 8, 128)
        dc, ds = dcos_ref[at, :].reshape(8, 8, 128), dsin_ref[at, :].reshape(8, 8, 128)
        out = pl.ds(pl.multiple_of(step * 128, 128), 128)
        for v in range(FRAME // 128):
            pair = jnp.stack([c, -s], axis=1).reshape(128, 128)
            table_ref[out, v * 128 : (v + 1) * 128] = pair.astype(jnp.bfloat16)
            if v < FRAME // 128 - 1:
                c, s = dc * c - ds * s, ds * c + dc * s
        return carry

    lax.fori_loop(0, LIVE // 64, turn, 0)

    def lanes(b, carry):
        lane = pl.multiple_of(b * 128, 128)

        def load(f, rows):
            return volt_ref[rows : rows + 16, pl.ds(pl.multiple_of(f * FRAME + lane, 128), 128)]

        def store(f, rows, value):
            at = (f - EARLY) * IN_DEV + rows
            late_ref[at : at + 16, pl.ds(lane, 128)] = value

        filter_block(window_ref, load, store, range(EARLY, FR_DEV), lane)
        return carry

    lax.fori_loop(0, FRAME // 128, lanes, 0)


def transposed_dot(a, b):
    return lax.dot_general(a, b, (((1,), (1,)), ((), ())), preferred_element_type=jnp.float32)


def spectra_into(table, early_ref, late_ref, out_ref):
    for n in range(FR_DEV * IN_DEV // 256):
        block = early_ref[...] if n == 0 else late_ref[(n - 1) * 256 : n * 256, :]
        out_ref[:, n * 256 : (n + 1) * 256] = transposed_dot(table, block).astype(jnp.bfloat16)


def second_kernel(halo_ref, volt_ref, window_ref, table_ref, late_ref, early_ref, out_ref):
    def lanes(b, carry):
        lane = pl.multiple_of(b * 128, 128)

        def load(f, rows):
            ref, g = (halo_ref, f + TAPS - 1) if f < 0 else (volt_ref, f)
            return ref[rows : rows + 16, pl.ds(pl.multiple_of(g * FRAME + lane, 128), 128)]

        def store(f, rows, value):
            at = f * IN_DEV + rows
            early_ref[at : at + 16, pl.ds(lane, 128)] = value

        filter_block(window_ref, load, store, range(EARLY), lane)
        return carry

    lax.fori_loop(0, FRAME // 128, lanes, 0)
    spectra_into(table_ref[...], early_ref, late_ref, out_ref)


def later_kernel(table_ref, early_ref, late_ref, out_ref):
    spectra_into(table_ref[...], early_ref, late_ref, out_ref)


def beam_kernel(recv_ref, place_ref, position_ref, sub_ref, out_ref, x_ref, part_ref, beam_ref, power_ref):
    p = pl.program_id(0)

    @pl.when(p == 0)
    def _():
        low = lax.broadcasted_iota(jnp.int32, (16, 128), 1) < IN_DEV

        def pairs(s, carry):
            lane = pl.multiple_of(s * 128, 128)
            for g in range(FR_DEV // 2):
                a = recv_ref[2 * s, :, g * 128 : (g + 1) * 128].astype(jnp.float32)
                b = recv_ref[2 * s + 1, :, g * 128 : (g + 1) * 128].astype(jnp.float32)
                even = jnp.where(low, a, pltpu.roll(b, 64, 1))
                odd = jnp.where(low, pltpu.roll(a, 64, 1), b)
                x_ref[g * 32 : g * 32 + 16, pl.ds(lane, 128)] = even.astype(jnp.bfloat16)
                x_ref[g * 32 + 16 : g * 32 + 32, pl.ds(lane, 128)] = odd.astype(jnp.bfloat16)
            return carry

        lax.fori_loop(0, N_FEED // 2, pairs, 0)

    for y in range(CYL):
        cells = jnp.dot(
            x_ref[...], place_ref[:, y * NS : (y + 1) * NS], preferred_element_type=jnp.float32
        ).astype(jnp.bfloat16)
        both = jnp.dot(cells, position_ref[...], preferred_element_type=jnp.float32)
        both = both.reshape(FR_DEV, 2, N_TM, 2 * NS)
        part_ref[y, :, 0] = both[:, 0, :, :NS] + both[:, 1, :, NS:]
        part_ref[y, :, 1] = both[:, 1, :, :NS] - both[:, 0, :, NS:]

    def join(f, carry):
        re = [part_ref[y, f, 0] for y in range(CYL)]
        im = [part_ref[y, f, 1] for y in range(CYL)]
        re_s, re_d = re[0] + re[2], re[0] - re[2]
        im_s, im_d = im[0] + im[2], im[0] - im[2]
        re_t, re_e = re[1] + re[3], re[1] - re[3]
        im_t, im_e = im[1] + im[3], im[1] - im[3]
        out_re = [re_s + re_t, re_d + im_e, re_s - re_t, re_d - im_e]
        out_im = [im_s + im_t, im_d - re_e, im_s - im_t, im_d + re_e]
        at = pl.ds(pl.multiple_of(f * 16, 16), 16)
        for e in range(CYL):
            value = jnp.concatenate([out_re[e], out_im[e]], axis=0) * 0.5
            beam_ref[at, e * NS : (e + 1) * NS] = value.astype(jnp.bfloat16)
        return carry

    lax.fori_loop(0, FR_DEV, join, 0)

    for e in range(CYL):
        at = slice(e * NS, (e + 1) * NS)
        up = jnp.dot(sub_ref[...], beam_ref[:, at], preferred_element_type=jnp.float32)
        power = up[:128] * up[:128] + up[128:] * up[128:]

        @pl.when(p == 0)
        def _():
            power_ref[:, at] = power

        @pl.when(p == 1)
        def _():
            out_ref[:, at] = (power_ref[:, at] + power).astype(jnp.bfloat16)


def cost(flops, nbytes):
    return pl.CostEstimate(flops=int(flops), bytes_accessed=int(nbytes), transcendentals=0)


def whole(shape, *index):
    index = index or (0,) * len(shape)
    return pl.BlockSpec(shape, lambda *_: index)


def local(voltages, feed_slot, channel_flags):
    bf16, f32 = jnp.bfloat16, jnp.float32
    history = voltages[:, (FR_DEV - TAPS + 1) * FRAME :]
    halo = lax.ppermute(history, "tm", [(i, i + 1) for i in range(N_TM - 1)])
    window = jnp.asarray(window_table())
    rows = FR_DEV * IN_DEV
    early_rows = EARLY * IN_DEV
    table, late = pl.pallas_call(
        first_kernel,
        name="table_and_filter",
        out_shape=[
            jax.ShapeDtypeStruct((2 * LIVE, FRAME), bf16),
            jax.ShapeDtypeStruct((rows - early_rows, FRAME), bf16),
        ],
        scratch_shapes=[pltpu.VMEM((LIVE, 128), f32)] * 4,
        compiler_params=pltpu.CompilerParams(vmem_limit_bytes=32 * MIB),
        cost_estimate=cost(9e9, 13 * MIB),
    )(channel_flags.reshape(1, CHANNELS), voltages, window)
    params = pltpu.CompilerParams(vmem_limit_bytes=32 * MIB)
    chunk_rows = 2 * LIVE // LIVE_DEV
    early, sent = pl.pallas_call(
        second_kernel,
        name="filter_and_spectra",
        grid=(1,),
        in_specs=[
            whole((IN_DEV, (TAPS - 1) * FRAME)),
            whole((IN_DEV, EARLY * FRAME)),
            whole((TAPS, FRAME)),
            whole((chunk_rows, FRAME)),
            whole((rows - early_rows, FRAME)),
        ],
        out_specs=[whole((early_rows, FRAME)), whole((chunk_rows, rows))],
        out_shape=[
            jax.ShapeDtypeStruct((early_rows, FRAME), bf16),
            jax.ShapeDtypeStruct((chunk_rows, rows), bf16),
        ],
        compiler_params=params,
        cost_estimate=cost(2.5e9, 8 * MIB),
    )(halo, voltages, window, table, late)
    chunks = [sent]
    for i in range(1, LIVE_DEV):
        chunks.append(
            pl.pallas_call(
                later_kernel,
                name="spectra",
                grid=(1,),
                in_specs=[
                    whole((chunk_rows, FRAME), i, 0),
                    whole((early_rows, FRAME)),
                    whole((rows - early_rows, FRAME)),
                ],
                out_specs=whole((chunk_rows, rows)),
                out_shape=jax.ShapeDtypeStruct((chunk_rows, rows), bf16),
                compiler_params=params,
                cost_estimate=cost(2.2e9, 8 * MIB),
            )(table, early, late)
        )
    inputs = N_FEED * IN_DEV
    place = (feed_slot[:, None] == jnp.arange(inputs, dtype=jnp.int32)[None, :]).astype(bf16)
    position = jnp.asarray(position_table(), dtype=bf16)
    sub = jnp.asarray(sub_channel_table(), dtype=bf16)
    powers = []
    for chunk in chunks:
        got = lax.all_to_all(
            chunk.reshape(N_FEED, 16, rows), "feed", split_axis=0, concat_axis=0, tiled=True
        )
        power = pl.pallas_call(
            beam_kernel,
            name="beams_and_power",
            grid=(2,),
            in_specs=[
                whole((N_FEED, 16, rows)),
                pl.BlockSpec((inputs, CYL * NS), lambda p: (0, p)),
                whole((NS, 2 * NS)),
                whole((256, 256)),
            ],
            out_specs=whole((128, CYL * NS)),
            out_shape=jax.ShapeDtypeStruct((128, CYL * NS), bf16),
            scratch_shapes=[
                pltpu.VMEM((256, inputs), bf16),
                pltpu.VMEM((CYL, FR_DEV, 2, N_TM, NS), f32),
                pltpu.VMEM((256, CYL * NS), bf16),
                pltpu.VMEM((128, CYL * NS), f32),
            ],
            compiler_params=pltpu.CompilerParams(vmem_limit_bytes=32 * MIB),
            cost_estimate=cost(3e9, 10 * MIB),
        )(got, place, position, sub)
        shared = lax.all_to_all(
            power.reshape(N_TM, UPCH, CYL * NS), "tm", split_axis=0, concat_axis=0, tiled=True
        )
        powers.append(shared)
    scale = 1.0 / (2.0 * N_TM * (FR_DEV // UPCH))
    return jnp.stack([jnp.sum(x.astype(f32), axis=0) * scale for x in powers])


def solution(mesh):
    in_specs = (P("feed", "tm"), P(), P())
    out_specs = P(("feed", "tm"), None, None)
    return jax.shard_map(local, mesh=mesh, in_specs=in_specs, out_specs=out_specs, check_vma=False)
```

```python
import math

import jax
import jax.numpy as jnp
import numpy as np
from jax import lax
from jax.experimental import pallas as pl
from jax.experimental.pallas import tpu as pltpu
from jax.sharding import PartitionSpec as P

CHANNELS = 1024
TAPS = 4
CYL = 4
NS = 256
UPCH = 16
FRAME = 2048
N_FEED = 32
N_TM = 8
IN_DEV = 64
FR_DEV = 16
LIVE_DEV = 3
LIVE = 768
OWNERS = 256
PAIRS = FR_DEV // 2
EARLY = 4
MIB = 1 << 20


def window_table():
    length = TAPS * FRAME
    sample = np.arange(length, dtype=np.float64)
    offset = (sample - length / 2 + 0.5) / FRAME
    taper = 0.5 - 0.5 * np.cos(2.0 * np.pi * (sample + 0.5) / length)
    return (np.sinc(offset) * taper).reshape(TAPS, FRAME).astype(np.float32)


def cos_sin(modulus, first, second):
    product = np.arange(first)[:, None] * np.arange(second)[None, :] % modulus
    angle = product * (2.0 * np.pi / modulus)
    scale = 1.0 / math.sqrt(modulus)
    return np.cos(angle) * scale, np.sin(angle) * scale


def position_table():
    cosine, sine = cos_sin(NS, NS, NS)
    return np.concatenate([cosine, sine], axis=1)


def sub_channel_table():
    cosine, sine = cos_sin(UPCH, UPCH, UPCH)
    real = np.stack([cosine, sine])
    imag = np.stack([-sine, cosine])
    both = np.stack([real, imag]).reshape(2, 2, PAIRS, 2, UPCH)
    return np.einsum("qrghk,bd->qbkdhrg", both, np.eye(N_TM)).reshape(256, 256)


def unit_circle(phase):
    quadrant = (phase + 256) >> 9
    x = (phase - (quadrant << 9)).astype(jnp.float32) * np.float32(2.0 * np.pi / FRAME)
    x2 = x * x
    c = 1.0 + x2 * (-0.5 + x2 * (1.0 / 24 + x2 * (-1.0 / 720 + x2 * (1.0 / 40320))))
    s = x * (1.0 + x2 * (-1.0 / 6 + x2 * (1.0 / 120 + x2 * (-1.0 / 5040 + x2 * (1.0 / 362880)))))
    odd = (quadrant & 1) == 1
    cos_mag = jnp.where(odd, s, c)
    sin_mag = jnp.where(odd, c, s)
    cosine = jnp.where(((quadrant + 1) & 2) == 2, -cos_mag, cos_mag)
    sine = jnp.where((quadrant & 2) == 2, -sin_mag, sin_mag)
    return cosine, sine


def filter_block(window_ref, load, store, frames, lane):
    taps = [window_ref[pl.ds(t, 1), pl.ds(lane, 128)] for t in range(TAPS)]
    for rows in range(0, IN_DEV, 16):
        held = {}
        for f in frames:
            total = None
            for t in range(TAPS):
                g = f - TAPS + 1 + t
                if g not in held:
                    held[g] = load(g, rows).astype(jnp.float32)
                term = taps[t] * held[g]
                total = term if total is None else total + term
            store(f, rows, total.astype(jnp.bfloat16))


def table_kernel(flags_ref, table_ref, cos_ref, sin_ref, dcos_ref, dsin_ref):
    rows = lax.broadcasted_iota(jnp.int32, (CHANNELS, CHANNELS), 0)
    cols = lax.broadcasted_iota(jnp.int32, (CHANNELS, CHANNELS), 1)
    upto = (rows <= cols).astype(jnp.float32).astype(jnp.bfloat16)
    flags = jnp.broadcast_to(flags_ref[...].astype(jnp.float32), (16, CHANNELS)).astype(jnp.bfloat16)
    count = jnp.dot(flags, upto, preferred_element_type=jnp.float32)[0:1].astype(jnp.int32)
    ones = jnp.ones((CHANNELS, 128), jnp.bfloat16)

    def place(step, carry):
        row = lax.broadcasted_iota(jnp.int32, (64, CHANNELS), 0) + step * 64
        rank = (row & (OWNERS - 1)) * LIVE_DEV + (row >> 8)
        below = (count <= rank).astype(jnp.float32).astype(jnp.bfloat16)
        channel = jnp.dot(below, ones, preferred_element_type=jnp.float32).astype(jnp.int32)
        at = pl.ds(pl.multiple_of(step * 64, 64), 64)
        lane = lax.broadcasted_iota(jnp.int32, (64, 128), 1)
        c, s = unit_circle((channel * lane) & (FRAME - 1))
        scale = np.float32(1.0 / math.sqrt(FRAME))
        cos_ref[at, :] = c * scale
        sin_ref[at, :] = s * scale
        c, s = unit_circle((channel * 128) & (FRAME - 1))
        dcos_ref[at, :] = c
        dsin_ref[at, :] = s
        return carry

    lax.fori_loop(0, LIVE // 64, place, 0)

    def turn(step, carry):
        at = pl.ds(pl.multiple_of(step * 64, 64), 64)
        c, s = cos_ref[at, :], sin_ref[at, :]
        dc, ds = dcos_ref[at, :], dsin_ref[at, :]
        out = (step >> 2) * (2 * OWNERS) + (step & 3) * 64
        re = pl.ds(pl.multiple_of(out, 64), 64)
        im = pl.ds(pl.multiple_of(out + OWNERS, 64), 64)
        for v in range(FRAME // 128):
            table_ref[re, v * 128 : (v + 1) * 128] = c.astype(jnp.bfloat16)
            table_ref[im, v * 128 : (v + 1) * 128] = (-s).astype(jnp.bfloat16)
            if v < FRAME // 128 - 1:
                c, s = dc * c - ds * s, ds * c + dc * s
        return carry

    lax.fori_loop(0, LIVE // 64, turn, 0)


def late_kernel(volt_ref, window_ref, late_ref):
    def lanes(b, carry):
        lane = pl.multiple_of(b * 128, 128)

        def load(f, rows):
            return volt_ref[rows : rows + 16, pl.ds(pl.multiple_of(f * FRAME + lane, 128), 128)]

        def store(f, rows, value):
            at = (f - EARLY) * IN_DEV + rows
            late_ref[at : at + 16, pl.ds(lane, 128)] = value

        filter_block(window_ref, load, store, range(EARLY, FR_DEV), lane)
        return carry

    lax.fori_loop(0, FRAME // 128, lanes, 0)


def transposed_dot(a, b):
    return lax.dot_general(a, b, (((1,), (1,)), ((), ())), preferred_element_type=jnp.float32)


def spectra_kernel(halo_ref, volt_ref, window_ref, table_ref, late_ref, out_ref, early_ref, wide_ref):
    @pl.when(pl.program_id(0) == 0)
    def _():
        def lanes(b, carry):
            lane = pl.multiple_of(b * 128, 128)

            def load(f, rows):
                ref, g = (halo_ref, f + TAPS - 1) if f < 0 else (volt_ref, f)
                return ref[rows : rows + 16, pl.ds(pl.multiple_of(g * FRAME + lane, 128), 128)]

            def store(f, rows, value):
                at = f * IN_DEV + rows
                early_ref[at : at + 16, pl.ds(lane, 128)] = value

            filter_block(window_ref, load, store, range(EARLY), lane)
            return carry

        lax.fori_loop(0, FRAME // 128, lanes, 0)

    for n in range(PAIRS // 2):
        block = early_ref[...] if n == 0 else late_ref[(n - 1) * 256 : n * 256, :]
        both = transposed_dot(table_ref[...], block)
        for r in range(2):
            for h in range(2):
                value = both[r * OWNERS : (r + 1) * OWNERS, h * 128 : (h + 1) * 128]
                wide_ref[pl.ds(r * PAIRS + 2 * n + h, OWNERS, 2 * PAIRS), :] = value
    out_ref[...] = wide_ref[...].reshape(OWNERS, 2 * PAIRS, 128).astype(jnp.bfloat16)


def beam_kernel(recv_ref, place_ref, position_ref, sub_ref, out_ref, x_ref, part_ref, beam_ref):
    low = lax.broadcasted_iota(jnp.int32, (2 * PAIRS, 128), 1) < IN_DEV

    def pairs(s, carry):
        lane = pl.multiple_of(s * 128, 128)
        for b in range(N_TM):
            one = recv_ref[2 * s * N_TM + b].astype(jnp.float32)
            two = recv_ref[(2 * s + 1) * N_TM + b].astype(jnp.float32)
            even = jnp.where(low, one, pltpu.roll(two, 64, 1))
            odd = jnp.where(low, pltpu.roll(one, 64, 1), two)
            x_ref[b * 32 : b * 32 + 16, pl.ds(lane, 128)] = even.astype(jnp.bfloat16)
            x_ref[b * 32 + 16 : b * 32 + 32, pl.ds(lane, 128)] = odd.astype(jnp.bfloat16)
        return carry

    lax.fori_loop(0, N_FEED // 2, pairs, 0)
    total = [None] * CYL
    for p in range(2):
        for y in range(CYL):
            at = slice((p * CYL + y) * NS, (p * CYL + y + 1) * NS)
            cells = jnp.dot(x_ref[...], place_ref[:, at], preferred_element_type=jnp.float32).astype(jnp.bfloat16)
            both = jnp.dot(cells, position_ref[...], preferred_element_type=jnp.float32)
            both = both.reshape(16, 2, PAIRS, 2 * NS)
            part_ref[y, :, 0] = both[:, 0, :, :NS] + both[:, 1, :, NS:]
            part_ref[y, :, 1] = both[:, 1, :, :NS] - both[:, 0, :, NS:]

        def join(f, carry):
            re = [part_ref[y, f, 0] for y in range(CYL)]
            im = [part_ref[y, f, 1] for y in range(CYL)]
            re_s, re_d = re[0] + re[2], re[0] - re[2]
            im_s, im_d = im[0] + im[2], im[0] - im[2]
            re_t, re_e = re[1] + re[3], re[1] - re[3]
            im_t, im_e = im[1] + im[3], im[1] - im[3]
            out_re = [re_s + re_t, re_d + im_e, re_s - re_t, re_d - im_e]
            out_im = [im_s + im_t, im_d - re_e, im_s - im_t, im_d + re_e]
            at = pl.ds(pl.multiple_of(f * 16, 16), 16)
            for e in range(CYL):
                value = jnp.concatenate([out_re[e], out_im[e]], axis=0) * 0.5
                beam_ref[at, e * NS : (e + 1) * NS] = value.astype(jnp.bfloat16)
            return carry

        lax.fori_loop(0, 16, join, 0)
        for e in range(CYL):
            up = jnp.dot(sub_ref[...], beam_ref[:, e * NS : (e + 1) * NS], preferred_element_type=jnp.float32)
            power = jnp.sum((up * up).reshape(2 * N_TM, UPCH, NS), axis=0)
            total[e] = power if p == 0 else total[e] + power
    for e in range(CYL):
        out_ref[0, :, e * NS : (e + 1) * NS] = total[e] * (1.0 / (2.0 * N_TM * (FR_DEV // UPCH)))


def cost(flops, nbytes):
    return pl.CostEstimate(flops=int(flops), bytes_accessed=int(nbytes), transcendentals=0)


def whole(shape, *index):
    index = index or (0,) * len(shape)
    return pl.BlockSpec(shape, lambda *_: index)


def local(voltages, feed_slot, channel_flags):
    bf16, f32 = jnp.bfloat16, jnp.float32
    history = voltages[:, (FR_DEV - TAPS + 1) * FRAME :]
    halo = lax.ppermute(history, "tm", [(i, i + 1) for i in range(N_TM - 1)])
    window = jnp.asarray(window_table())
    late_rows = (FR_DEV - EARLY) * IN_DEV
    early_rows = EARLY * IN_DEV
    params = pltpu.CompilerParams(vmem_limit_bytes=32 * MIB)
    table = pl.pallas_call(
        table_kernel,
        name="channel_table",
        out_shape=jax.ShapeDtypeStruct((2 * LIVE, FRAME), bf16),
        scratch_shapes=[pltpu.VMEM((LIVE, 128), f32)] * 4,
        compiler_params=params,
        cost_estimate=cost(4e9, 6 * MIB),
    )(channel_flags.reshape(1, CHANNELS))
    late = pl.pallas_call(
        late_kernel,
        name="filter",
        out_shape=jax.ShapeDtypeStruct((late_rows, FRAME), bf16),
        compiler_params=params,
        cost_estimate=cost(4e9, 7 * MIB),
    )(voltages, window)
    sent = pl.pallas_call(
        spectra_kernel,
        name="spectra",
        grid=(LIVE_DEV,),
        in_specs=[
            whole((IN_DEV, (TAPS - 1) * FRAME)),
            whole((IN_DEV, EARLY * FRAME)),
            whole((TAPS, FRAME)),
            pl.BlockSpec((2 * OWNERS, FRAME), lambda c: (c, 0)),
            whole((late_rows, FRAME)),
        ],
        out_specs=pl.BlockSpec((OWNERS, 2 * PAIRS, 128), lambda c: (0, c, 0)),
        out_shape=pltpu.HBM((OWNERS, LIVE_DEV * 2 * PAIRS, 128), bf16),
        scratch_shapes=[
            pltpu.VMEM((early_rows, FRAME), bf16),
            pltpu.VMEM((OWNERS * 2 * PAIRS, 128), f32),
        ],
        compiler_params=params,
        cost_estimate=cost(7e9, 14 * MIB),
    )(halo, voltages, window, table, late)
    got = lax.all_to_all(sent, ("feed", "tm"), split_axis=0, concat_axis=0, tiled=True)
    inputs = N_FEED * IN_DEV
    place = (feed_slot[:, None] == jnp.arange(inputs, dtype=jnp.int32)[None, :]).astype(bf16)
    return pl.pallas_call(
        beam_kernel,
        name="beams_and_power",
        grid=(LIVE_DEV,),
        in_specs=[
            pl.BlockSpec((OWNERS, 2 * PAIRS, 128), lambda c: (0, c, 0)),
            whole((inputs, inputs)),
            whole((NS, 2 * NS)),
            whole((256, 256)),
        ],
        out_specs=pl.BlockSpec((1, UPCH, CYL * NS), lambda c: (c, 0, 0)),
        out_shape=jax.ShapeDtypeStruct((LIVE_DEV, UPCH, CYL * NS), f32),
        scratch_shapes=[
            pltpu.VMEM((256, inputs), bf16),
            pltpu.VMEM((CYL, 16, 2, PAIRS, NS), f32),
            pltpu.VMEM((256, CYL * NS), bf16),
        ],
        compiler_params=pltpu.CompilerParams(vmem_limit_bytes=36 * MIB),
        cost_estimate=cost(9e9, 14 * MIB),
    )(got, place, jnp.asarray(position_table(), dtype=bf16), jnp.asarray(sub_channel_table(), dtype=bf16))


def solution(mesh):
    in_specs = (P("feed", "tm"), P(), P())
    out_specs = P(("feed", "tm"), None, None)
    return jax.shard_map(local, mesh=mesh, in_specs=in_specs, out_specs=out_specs, check_vma=False)
```

```python
import math

import jax
import jax.numpy as jnp
import numpy as np
from jax import lax
from jax.experimental import pallas as pl
from jax.experimental.pallas import tpu as pltpu
from jax.sharding import PartitionSpec as P

CHANNELS = 1024
TAPS = 4
CYL = 4
NS = 256
UPCH = 16
FRAME = 2048
N_FEED = 32
N_TM = 8
IN_DEV = 64
FR_DEV = 16
LIVE_DEV = 3
LIVE = 768
OWNERS = 256
PAIRS = FR_DEV // 2
EARLY = 4
MIB = 1 << 20


def window_table():
    length = TAPS * FRAME
    sample = np.arange(length, dtype=np.float64)
    offset = (sample - length / 2 + 0.5) / FRAME
    taper = 0.5 - 0.5 * np.cos(2.0 * np.pi * (sample + 0.5) / length)
    return (np.sinc(offset) * taper).reshape(TAPS, FRAME).astype(np.float32)


def cos_sin(modulus, first, second):
    product = np.arange(first)[:, None] * np.arange(second)[None, :] % modulus
    angle = product * (2.0 * np.pi / modulus)
    scale = 1.0 / math.sqrt(modulus)
    return np.cos(angle) * scale, np.sin(angle) * scale


def position_table():
    cosine, sine = cos_sin(NS, NS, NS)
    return np.block([[cosine, -sine], [sine, cosine]])


def sub_channel_table():
    cosine, sine = cos_sin(UPCH, UPCH, UPCH)
    real = np.stack([cosine, sine])
    imag = np.stack([-sine, cosine])
    both = np.stack([real, imag]).reshape(2, 2, PAIRS, 2, UPCH)
    return np.einsum("qrghk,bd->qbkdhrg", both, np.eye(N_TM)).reshape(256, 256)


def unit_circle(phase):
    quadrant = (phase + 256) >> 9
    x = (phase - (quadrant << 9)).astype(jnp.float32) * np.float32(2.0 * np.pi / FRAME)
    x2 = x * x
    c = 1.0 + x2 * (-0.5 + x2 * (1.0 / 24 + x2 * (-1.0 / 720 + x2 * (1.0 / 40320))))
    s = x * (1.0 + x2 * (-1.0 / 6 + x2 * (1.0 / 120 + x2 * (-1.0 / 5040 + x2 * (1.0 / 362880)))))
    odd = (quadrant & 1) == 1
    cos_mag = jnp.where(odd, s, c)
    sin_mag = jnp.where(odd, c, s)
    cosine = jnp.where(((quadrant + 1) & 2) == 2, -cos_mag, cos_mag)
    sine = jnp.where((quadrant & 2) == 2, -sin_mag, sin_mag)
    return cosine, sine


def filter_block(window_ref, load, store, frames, lane):
    taps = [window_ref[pl.ds(t, 1), pl.ds(lane, 128)] for t in range(TAPS)]
    for rows in range(0, IN_DEV, 16):
        held = {}
        for f in frames:
            total = None
            for t in range(TAPS):
                g = f - TAPS + 1 + t
                if g not in held:
                    held[g] = load(g, rows).astype(jnp.float32)
                term = taps[t] * held[g]
                total = term if total is None else total + term
            store(f, rows, total.astype(jnp.bfloat16))


def table_kernel(flags_ref, table_ref, cos_ref, sin_ref, dcos_ref, dsin_ref, sign_ref):
    lane = lax.broadcasted_iota(jnp.int32, (64, 128), 1)
    upto = (lax.broadcasted_iota(jnp.int32, (128, 128), 0) <= lax.broadcasted_iota(jnp.int32, (128, 128), 1)).astype(
        jnp.float32
    )
    ones = jnp.ones((128, 128), jnp.float32)
    sums = jnp.concatenate([upto, ones], axis=1).astype(jnp.bfloat16)
    ones = ones.astype(jnp.bfloat16)
    flags = flags_ref[...].astype(jnp.float32)
    flags = jnp.concatenate([flags, jnp.zeros_like(flags)], axis=0).astype(jnp.bfloat16)
    count = jnp.dot(flags, sums, preferred_element_type=jnp.float32)
    earlier = jnp.zeros((1, 128), jnp.float32)
    counts = []
    for r in range(CHANNELS // 128):
        counts.append((count[r : r + 1, :128] + earlier).astype(jnp.int32))
        earlier = earlier + count[r : r + 1, 128:]

    def place(step, carry):
        row = lax.broadcasted_iota(jnp.int32, (64, 128), 0) + step * 64
        rank = (row & (OWNERS - 1)) * LIVE_DEV + (row >> 8)
        below = sum((c <= rank).astype(jnp.float32) for c in counts).astype(jnp.bfloat16)
        channel = jnp.dot(below, ones, preferred_element_type=jnp.float32).astype(jnp.int32)
        at = pl.ds(pl.multiple_of(step * 64, 64), 64)
        c, s = unit_circle((channel * lane) & (FRAME - 1))
        scale = np.float32(1.0 / math.sqrt(FRAME))
        cos_ref[at, :] = c * scale
        sin_ref[at, :] = s * scale
        c, s = unit_circle((channel * 128) & (FRAME - 1))
        dcos_ref[at, :] = c
        dsin_ref[at, :] = s
        sign_ref[at, :] = (1 - 2 * (channel & 1)).astype(jnp.float32)
        return carry

    lax.fori_loop(0, LIVE // 64, place, 0)

    def turn(step, carry):
        at = pl.ds(pl.multiple_of(step * 64, 64), 64)
        c, s = cos_ref[at, :], sin_ref[at, :]
        dc, ds = dcos_ref[at, :], dsin_ref[at, :]
        sign = sign_ref[at, :].astype(jnp.bfloat16)
        out = (step >> 2) * (2 * OWNERS) + (step & 3) * 64
        re = pl.ds(pl.multiple_of(out, 64), 64)
        im = pl.ds(pl.multiple_of(out + OWNERS, 64), 64)
        half = FRAME // 256
        for v in range(half):
            cb, sb = c.astype(jnp.bfloat16), (-s).astype(jnp.bfloat16)
            table_ref[re, v * 128 : (v + 1) * 128] = cb
            table_ref[im, v * 128 : (v + 1) * 128] = sb
            table_ref[re, (v + half) * 128 : (v + half + 1) * 128] = cb * sign
            table_ref[im, (v + half) * 128 : (v + half + 1) * 128] = sb * sign
            if v < half - 1:
                c, s = dc * c - ds * s, ds * c + dc * s
        return carry

    lax.fori_loop(0, LIVE // 64, turn, 0)


def late_kernel(volt_ref, window_ref, _, late_ref):
    def lanes(b, carry):
        lane = pl.multiple_of(b * 128, 128)

        def load(f, rows):
            return volt_ref[rows : rows + 16, pl.ds(pl.multiple_of(f * FRAME + lane, 128), 128)]

        def store(f, rows, value):
            at = (f - EARLY) * IN_DEV + rows
            late_ref[at : at + 16, pl.ds(lane, 128)] = value

        filter_block(window_ref, load, store, range(EARLY, FR_DEV), lane)
        return carry

    lax.fori_loop(0, FRAME // 128, lanes, 0)


def transposed_dot(a, b):
    return lax.dot_general(a, b, (((1,), (1,)), ((), ())), preferred_element_type=jnp.float32)


def spectra_kernel(halo_ref, volt_ref, window_ref, table_ref, late_ref, out_ref, early_ref, wide_ref):
    @pl.when(pl.program_id(0) == 0)
    def _():
        def lanes(b, carry):
            lane = pl.multiple_of(b * 128, 128)

            def load(f, rows):
                ref, g = (halo_ref, f + TAPS - 1) if f < 0 else (volt_ref, f)
                return ref[rows : rows + 16, pl.ds(pl.multiple_of(g * FRAME + lane, 128), 128)]

            def store(f, rows, value):
                at = f * IN_DEV + rows
                early_ref[at : at + 16, pl.ds(lane, 128)] = value

            filter_block(window_ref, load, store, range(EARLY), lane)
            return carry

        lax.fori_loop(0, FRAME // 128, lanes, 0)

    table = table_ref[pl.ds(pl.multiple_of(pl.program_id(0) * 2 * OWNERS, 2 * OWNERS), 2 * OWNERS), :]
    for n in range(PAIRS // 2):
        block = early_ref[...] if n == 0 else late_ref[(n - 1) * 256 : n * 256, :]
        both = transposed_dot(table, block)
        for r in range(2):
            for h in range(2):
                value = both[r * OWNERS : (r + 1) * OWNERS, h * 128 : (h + 1) * 128]
                wide_ref[pl.ds(r * PAIRS + 2 * n + h, OWNERS, 2 * PAIRS), :] = value
    out_ref[...] = wide_ref[...].reshape(OWNERS, 2 * PAIRS, 128).astype(jnp.bfloat16)


def beam_kernel(recv_ref, slot_ref, position_ref, sub_ref, out_ref, x_ref, place_ref, cell_ref, part_ref, beam_ref):
    low = lax.broadcasted_iota(jnp.int32, (2 * PAIRS, 128), 1) < IN_DEV
    groups = 2 * CYL

    def pairs(s, carry):
        lane = pl.multiple_of(s * 128, 128)
        for c in range(LIVE_DEV):
            for b in range(N_TM):
                part = slice(c * 2 * PAIRS, (c + 1) * 2 * PAIRS)
                one = recv_ref[2 * s * N_TM + b, part].astype(jnp.float32)
                two = recv_ref[(2 * s + 1) * N_TM + b, part].astype(jnp.float32)
                even = jnp.where(low, one, pltpu.roll(two, 64, 1))
                odd = jnp.where(low, pltpu.roll(one, 64, 1), two)
                row = c * 256 + b * 32
                x_ref[row : row + 16, pl.ds(lane, 128)] = even.astype(jnp.bfloat16)
                x_ref[row + 16 : row + 32, pl.ds(lane, 128)] = odd.astype(jnp.bfloat16)
        return carry

    lax.fori_loop(0, N_FEED // 2, pairs, 0)
    slot = jnp.concatenate([slot_ref[...]] * 2, axis=1)
    for i in range(groups):
        want = lax.broadcasted_iota(jnp.int32, slot.shape, 1) + i * NS
        place_ref[i % 2] = (slot == want).astype(jnp.float32).astype(jnp.bfloat16)
        cells = jnp.dot(x_ref[...], place_ref[i % 2], preferred_element_type=jnp.float32)
        cells = cells.reshape(-1, 2, PAIRS, NS)
        both = [cells[:, r].reshape(-1, NS) for r in range(2)]
        cell_ref[i] = jnp.concatenate(both, axis=1).astype(jnp.bfloat16)
    for i in range(groups):
        part_ref[i] = jnp.dot(cell_ref[i], position_ref[...], preferred_element_type=jnp.float32)
    for p in range(2):

        def join(f, carry):
            rows = pl.ds(pl.multiple_of(f * PAIRS, PAIRS), PAIRS)
            re = [part_ref[p * CYL + y, rows, :NS] for y in range(CYL)]
            im = [part_ref[p * CYL + y, rows, NS:] for y in range(CYL)]
            re_s, re_d = re[0] + re[2], re[0] - re[2]
            im_s, im_d = im[0] + im[2], im[0] - im[2]
            re_t, re_e = re[1] + re[3], re[1] - re[3]
            im_t, im_e = im[1] + im[3], im[1] - im[3]
            out_re = [re_s + re_t, re_d + im_e, re_s - re_t, re_d - im_e]
            out_im = [im_s + im_t, im_d - re_e, im_s - im_t, im_d + re_e]
            at = pl.ds(pl.multiple_of(f * 2 * PAIRS, 2 * PAIRS), 2 * PAIRS)
            for e in range(CYL):
                value = jnp.concatenate([out_re[e], out_im[e]], axis=0) * 0.5
                beam_ref[p, at, e * NS : (e + 1) * NS] = value.astype(jnp.bfloat16)
            return carry

        lax.fori_loop(0, LIVE_DEV * 16, join, 0, unroll=2)
    for c in range(LIVE_DEV):
        for e in range(CYL):
            total = None
            for p in range(2):
                beams = beam_ref[p, c * 256 : (c + 1) * 256, e * NS : (e + 1) * NS]
                up = jnp.dot(sub_ref[...], beams, preferred_element_type=jnp.float32)
                power = jnp.sum((up * up).reshape(2 * N_TM, UPCH, NS), axis=0)
                total = power if p == 0 else total + power
            out_ref[c, :, e * NS : (e + 1) * NS] = total * (1.0 / (2.0 * N_TM * (FR_DEV // UPCH)))


def cost(flops, nbytes):
    return pl.CostEstimate(flops=int(flops), bytes_accessed=int(nbytes), transcendentals=0)


def whole(shape, *index):
    index = index or (0,) * len(shape)
    return pl.BlockSpec(shape, lambda *_: index)


def local(voltages, feed_slot, channel_flags):
    bf16, f32 = jnp.bfloat16, jnp.float32
    history = voltages[:, (FR_DEV - TAPS + 1) * FRAME :]
    halo = lax.ppermute(history, "tm", [(i, i + 1) for i in range(N_TM - 1)])
    window = jnp.asarray(window_table())
    in_vmem = pl.BlockSpec(memory_space=pltpu.VMEM)
    late_rows = (FR_DEV - EARLY) * IN_DEV
    early_rows = EARLY * IN_DEV
    params = pltpu.CompilerParams(vmem_limit_bytes=32 * MIB)
    table = pl.pallas_call(
        table_kernel,
        name="channel_table",
        out_shape=jax.ShapeDtypeStruct((2 * LIVE, FRAME), bf16),
        scratch_shapes=[pltpu.VMEM((LIVE, 128), f32)] * 5,
        compiler_params=params,
        cost_estimate=cost(4e9, 6 * MIB),
    )(channel_flags.reshape(CHANNELS // 128, 128))
    late = pl.pallas_call(
        late_kernel,
        name="filter",
        in_specs=[in_vmem, in_vmem, pl.BlockSpec(memory_space=pl.ANY)],
        out_shape=jax.ShapeDtypeStruct((late_rows, FRAME), bf16),
        compiler_params=params,
        cost_estimate=cost(4e9, 7 * MIB),
    )(voltages, window, table)
    sent = pl.pallas_call(
        spectra_kernel,
        name="spectra",
        grid=(LIVE_DEV,),
        in_specs=[
            in_vmem,
            whole((IN_DEV, EARLY * FRAME)),
            in_vmem,
            in_vmem,
            in_vmem,
        ],
        out_specs=pl.BlockSpec((OWNERS, 2 * PAIRS, 128), lambda c: (0, c, 0)),
        out_shape=pltpu.HBM((OWNERS, LIVE_DEV * 2 * PAIRS, 128), bf16),
        scratch_shapes=[
            pltpu.VMEM((early_rows, FRAME), bf16),
            pltpu.VMEM((OWNERS * 2 * PAIRS, 128), f32),
        ],
        compiler_params=params,
        cost_estimate=cost(7e9, 14 * MIB),
    )(halo, voltages, window, table, late)
    got = lax.all_to_all(sent, ("feed", "tm"), split_axis=0, concat_axis=0, tiled=True)
    inputs = N_FEED * IN_DEV
    rows = LIVE_DEV * 256
    return pl.pallas_call(
        beam_kernel,
        name="beams_and_power",
        in_specs=[in_vmem] * 4,
        out_specs=in_vmem,
        out_shape=jax.ShapeDtypeStruct((LIVE_DEV, UPCH, CYL * NS), f32),
        scratch_shapes=[
            pltpu.VMEM((rows, inputs), bf16),
            pltpu.VMEM((2, inputs, NS), bf16),
            pltpu.VMEM((2 * CYL, rows // 2, 2 * NS), bf16),
            pltpu.VMEM((2 * CYL, rows // 2, 2 * NS), f32),
            pltpu.VMEM((2, rows, CYL * NS), bf16),
        ],
        compiler_params=pltpu.CompilerParams(vmem_limit_bytes=36 * MIB),
        cost_estimate=cost(9e9, 6 * MIB),
    )(
        got,
        jnp.broadcast_to(feed_slot[:, None], (inputs, 128)),
        jnp.asarray(position_table(), dtype=bf16),
        jnp.asarray(sub_channel_table(), dtype=bf16),
    )


def solution(mesh):
    in_specs = (P("feed", "tm"), P(), P())
    out_specs = P(("feed", "tm"), None, None)
    return jax.shard_map(local, mesh=mesh, in_specs=in_specs, out_specs=out_specs, check_vma=False)
```

```python
import math

import jax
import jax.numpy as jnp
import numpy as np
from jax import lax
from jax.experimental import pallas as pl
from jax.experimental.pallas import tpu as pltpu
from jax.sharding import PartitionSpec as P

CHANNELS = 1024
TAPS = 4
CYL = 4
NS = 256
UPCH = 16
FRAME = 2048
N_FEED = 32
N_TM = 8
IN_DEV = 64
FR_DEV = 16
LIVE_DEV = 3
LIVE = 768
OWNERS = 256
PAIRS = FR_DEV // 2
EARLY = 4
MIB = 1 << 20


def window_table():
    length = TAPS * FRAME
    sample = np.arange(length, dtype=np.float64)
    offset = (sample - length / 2 + 0.5) / FRAME
    taper = 0.5 - 0.5 * np.cos(2.0 * np.pi * (sample + 0.5) / length)
    return (np.sinc(offset) * taper).reshape(TAPS, FRAME).astype(np.float32)


def cos_sin(modulus, first, second):
    product = np.arange(first)[:, None] * np.arange(second)[None, :] % modulus
    angle = product * (2.0 * np.pi / modulus)
    scale = 1.0 / math.sqrt(modulus)
    return np.cos(angle) * scale, np.sin(angle) * scale


def position_table():
    cosine, sine = cos_sin(NS, NS, NS)
    return np.block([[cosine, -sine], [sine, cosine]])


def sub_channel_table():
    cosine, sine = cos_sin(UPCH, UPCH, UPCH)
    real = np.stack([cosine, sine])
    imag = np.stack([-sine, cosine])
    both = np.stack([real, imag]).reshape(2, 2, PAIRS, 2, UPCH)
    return np.einsum("qrghk,bd->qbkdhrg", both, np.eye(N_TM)).reshape(256, 256)


def unit_circle(phase):
    quadrant = (phase + 256) >> 9
    x = (phase - (quadrant << 9)).astype(jnp.float32) * np.float32(2.0 * np.pi / FRAME)
    x2 = x * x
    c = 1.0 + x2 * (-0.5 + x2 * (1.0 / 24 + x2 * (-1.0 / 720 + x2 * (1.0 / 40320))))
    s = x * (1.0 + x2 * (-1.0 / 6 + x2 * (1.0 / 120 + x2 * (-1.0 / 5040 + x2 * (1.0 / 362880)))))
    odd = (quadrant & 1) == 1
    cos_mag = jnp.where(odd, s, c)
    sin_mag = jnp.where(odd, c, s)
    cosine = jnp.where(((quadrant + 1) & 2) == 2, -cos_mag, cos_mag)
    sine = jnp.where((quadrant & 2) == 2, -sin_mag, sin_mag)
    return cosine, sine


def fold_frames(window_ref, load, frames, even_ref, odd_ref, middle_ref, last_ref):
    lane = lax.broadcasted_iota(jnp.int32, (16, 128), 1)
    back = (128 - lane) & 127
    last_ref[...] = jnp.zeros_like(last_ref)

    def piece(v, carry):
        sides = [pl.multiple_of(v * 128, 128), pl.multiple_of((FRAME // 128 - 1 - v) * 128, 128)]
        taps = [[window_ref[pl.ds(t, 1), pl.ds(side, 128)] for t in range(TAPS)] for side in sides]
        for rows in range(0, IN_DEV, 16):
            held = [{}, {}]
            for n, f in enumerate(frames):
                total = [None, None]
                for j in range(2):
                    for t in range(TAPS):
                        g = f - TAPS + 1 + t
                        if g not in held[j]:
                            held[j][g] = load(g, rows, sides[j]).astype(jnp.float32)
                        term = taps[j][t] * held[j][g]
                        total[j] = term if t == 0 else total[j] + term
                at = slice(n * IN_DEV + rows, n * IN_DEV + rows + 16)
                turned = jnp.take_along_axis(total[1], back, axis=1, mode="promise_in_bounds")
                mirror = jnp.where(lane == 0, last_ref[at, :], turned)
                last_ref[at, :] = turned
                even_ref[at, pl.ds(sides[0], 128)] = (total[0] + mirror).astype(jnp.bfloat16)
                odd_ref[at, pl.ds(sides[0], 128)] = (total[0] - mirror).astype(jnp.bfloat16)
                middle_ref[at, :] = total[1].astype(jnp.bfloat16)
        return carry

    lax.fori_loop(0, FRAME // 256, piece, 0)


def table_kernel(flags_ref, table_ref, sign_ref, cos_ref, sin_ref, dcos_ref, dsin_ref):
    lane = lax.broadcasted_iota(jnp.int32, (64, 128), 1)
    upto = (lax.broadcasted_iota(jnp.int32, (128, 128), 0) <= lax.broadcasted_iota(jnp.int32, (128, 128), 1)).astype(
        jnp.float32
    )
    ones = jnp.ones((128, 128), jnp.float32)
    sums = jnp.concatenate([upto, ones], axis=1).astype(jnp.bfloat16)
    ones = ones.astype(jnp.bfloat16)
    flags = flags_ref[...].astype(jnp.float32)
    flags = jnp.concatenate([flags, jnp.zeros_like(flags)], axis=0).astype(jnp.bfloat16)
    count = jnp.dot(flags, sums, preferred_element_type=jnp.float32)
    earlier = jnp.zeros((1, 128), jnp.float32)
    counts = []
    for r in range(CHANNELS // 128):
        counts.append((count[r : r + 1, :128] + earlier).astype(jnp.int32))
        earlier = earlier + count[r : r + 1, 128:]

    def place(step, carry):
        row = lax.broadcasted_iota(jnp.int32, (64, 128), 0) + step * 64
        rank = (row & (OWNERS - 1)) * LIVE_DEV + (row >> 8)
        below = sum((c <= rank).astype(jnp.float32) for c in counts).astype(jnp.bfloat16)
        channel = jnp.dot(below, ones, preferred_element_type=jnp.float32).astype(jnp.int32)
        at = pl.ds(pl.multiple_of(step * 64, 64), 64)
        c, s = unit_circle((channel * lane) & (FRAME - 1))
        scale = np.float32(1.0 / math.sqrt(FRAME))
        cos_ref[at, :] = c * scale
        sin_ref[at, :] = s * scale
        c, s = unit_circle((channel * 128) & (FRAME - 1))
        dcos_ref[at, :] = c
        dsin_ref[at, :] = s
        sign = (1 - 2 * (channel & 1)).astype(jnp.float32) * scale
        sign_ref[at, :] = jnp.where(lane == 0, sign, 0.0).astype(jnp.bfloat16)
        return carry

    lax.fori_loop(0, LIVE // 64, place, 0)

    def turn(step, carry):
        at = pl.ds(pl.multiple_of(step * 64, 64), 64)
        c, s = cos_ref[at, :], sin_ref[at, :]
        dc, ds = dcos_ref[at, :], dsin_ref[at, :]
        for v in range(FRAME // 256):
            table_ref[0, at, v * 128 : (v + 1) * 128] = c.astype(jnp.bfloat16)
            table_ref[1, at, v * 128 : (v + 1) * 128] = (-s).astype(jnp.bfloat16)
            if v < FRAME // 256 - 1:
                c, s = dc * c - ds * s, ds * c + dc * s
        return carry

    lax.fori_loop(0, LIVE // 64, turn, 0)


def late_kernel(volt_ref, window_ref, _, even_ref, odd_ref, middle_ref, last_ref):
    def load(f, rows, lane):
        return volt_ref[rows : rows + 16, pl.ds(pl.multiple_of(f * FRAME + lane, 128), 128)]

    fold_frames(window_ref, load, range(EARLY, FR_DEV), even_ref, odd_ref, middle_ref, last_ref)


def transposed_dot(a, b):
    return lax.dot_general(a, b, (((1,), (1,)), ((), ())), preferred_element_type=jnp.float32)


def put_spectra(table, sign, even, odd, middle, wide_ref, first):
    real = transposed_dot(table[0], even) + transposed_dot(sign, middle)
    for r, value in enumerate((real, transposed_dot(table[1], odd))):
        for h in range(2):
            wide_ref[pl.ds(r * PAIRS + first + h, OWNERS, 2 * PAIRS), :] = value[:, h * 128 : (h + 1) * 128]


def late_spectra_kernel(table_ref, sign_ref, even_ref, odd_ref, middle_ref, wide_ref):
    for c in range(LIVE_DEV):
        at = slice(c * OWNERS, (c + 1) * OWNERS)
        for n in range(PAIRS // 2 - 1):
            rows = slice(n * 256, (n + 1) * 256)
            table = table_ref[0, at, :], table_ref[1, at, :]
            sources = even_ref[rows, :], odd_ref[rows, :], middle_ref[rows, :]
            put_spectra(table, sign_ref[at, :], *sources, wide_ref.at[c], 2 * (n + 1))


def spectra_kernel(
    halo_ref, volt_ref, window_ref, table_ref, sign_ref, late_ref, out_ref, even_ref, odd_ref, middle_ref, last_ref, wide_ref
):
    c = pl.program_id(0)

    @pl.when(c == 0)
    def _():
        def load(f, rows, lane):
            ref, g = (halo_ref, f + TAPS - 1) if f < 0 else (volt_ref, f)
            return ref[rows : rows + 16, pl.ds(pl.multiple_of(g * FRAME + lane, 128), 128)]

        fold_frames(window_ref, load, range(EARLY), even_ref, odd_ref, middle_ref, last_ref)

    at = pl.ds(pl.multiple_of(c * OWNERS, OWNERS), OWNERS)
    table = table_ref[0, at, :], table_ref[1, at, :]
    put_spectra(table, sign_ref[at, :], even_ref[...], odd_ref[...], middle_ref[...], wide_ref, 0)

    def join(step, carry):
        rows = pl.ds(pl.multiple_of(step * 256, 256), 256)
        early = lax.broadcasted_iota(jnp.int32, (256, 128), 0) & (PAIRS - 1) < EARLY // 2
        value = jnp.where(early, wide_ref[rows, :], late_ref[c, rows, :])
        owners = pl.ds(pl.multiple_of(step * 16, 16), 16)
        out_ref[owners] = value.reshape(16, 2 * PAIRS, 128).astype(jnp.bfloat16)
        return carry

    lax.fori_loop(0, OWNERS // 16, join, 0)


def beam_kernel(recv_ref, slot_ref, position_ref, sub_ref, out_ref, x_ref, place_ref, cell_ref, part_ref, beam_ref):
    low = lax.broadcasted_iota(jnp.int32, (2 * PAIRS, 128), 1) < IN_DEV
    groups = 2 * CYL

    def pairs(s, carry):
        lane = pl.multiple_of(s * 128, 128)
        for c in range(LIVE_DEV):
            for b in range(N_TM):
                part = slice(c * 2 * PAIRS, (c + 1) * 2 * PAIRS)
                one = recv_ref[2 * s * N_TM + b, part].astype(jnp.float32)
                two = recv_ref[(2 * s + 1) * N_TM + b, part].astype(jnp.float32)
                even = jnp.where(low, one, pltpu.roll(two, 64, 1))
                odd = jnp.where(low, pltpu.roll(one, 64, 1), two)
                row = c * 256 + b * 32
                x_ref[row : row + 16, pl.ds(lane, 128)] = even.astype(jnp.bfloat16)
                x_ref[row + 16 : row + 32, pl.ds(lane, 128)] = odd.astype(jnp.bfloat16)
        return carry

    lax.fori_loop(0, N_FEED // 2, pairs, 0)
    slot = jnp.concatenate([slot_ref[...]] * 2, axis=1)
    for i in range(groups):
        want = lax.broadcasted_iota(jnp.int32, slot.shape, 1) + i * NS
        place_ref[i % 2] = (slot == want).astype(jnp.float32).astype(jnp.bfloat16)
        cells = jnp.dot(x_ref[...], place_ref[i % 2], preferred_element_type=jnp.float32)
        cells = cells.reshape(-1, 2, PAIRS, NS)
        both = [cells[:, r].reshape(-1, NS) for r in range(2)]
        cell_ref[i] = jnp.concatenate(both, axis=1).astype(jnp.bfloat16)
    for i in range(groups):
        part_ref[i] = jnp.dot(cell_ref[i], position_ref[...], preferred_element_type=jnp.float32)
    for p in range(2):

        def join(f, carry):
            rows = pl.ds(pl.multiple_of(f * PAIRS, PAIRS), PAIRS)
            re = [part_ref[p * CYL + y, rows, :NS] for y in range(CYL)]
            im = [part_ref[p * CYL + y, rows, NS:] for y in range(CYL)]
            re_s, re_d = re[0] + re[2], re[0] - re[2]
            im_s, im_d = im[0] + im[2], im[0] - im[2]
            re_t, re_e = re[1] + re[3], re[1] - re[3]
            im_t, im_e = im[1] + im[3], im[1] - im[3]
            out_re = [re_s + re_t, re_d + im_e, re_s - re_t, re_d - im_e]
            out_im = [im_s + im_t, im_d - re_e, im_s - im_t, im_d + re_e]
            at = pl.ds(pl.multiple_of(f * 2 * PAIRS, 2 * PAIRS), 2 * PAIRS)
            for e in range(CYL):
                value = jnp.concatenate([out_re[e], out_im[e]], axis=0) * 0.5
                beam_ref[p, at, e * NS : (e + 1) * NS] = value.astype(jnp.bfloat16)
            return carry

        lax.fori_loop(0, LIVE_DEV * 16, join, 0, unroll=2)
    for c in range(LIVE_DEV):
        for e in range(CYL):
            total = None
            for p in range(2):
                beams = beam_ref[p, c * 256 : (c + 1) * 256, e * NS : (e + 1) * NS]
                up = jnp.dot(sub_ref[...], beams, preferred_element_type=jnp.float32)
                power = jnp.sum((up * up).reshape(2 * N_TM, UPCH, NS), axis=0)
                total = power if p == 0 else total + power
            out_ref[c, :, e * NS : (e + 1) * NS] = total * (1.0 / (2.0 * N_TM * (FR_DEV // UPCH)))


def cost(flops, nbytes):
    return pl.CostEstimate(flops=int(flops), bytes_accessed=int(nbytes), transcendentals=0)


def whole(shape, *index):
    index = index or (0,) * len(shape)
    return pl.BlockSpec(shape, lambda *_: index)


def local(voltages, feed_slot, channel_flags):
    bf16, f32 = jnp.bfloat16, jnp.float32
    history = voltages[:, (FR_DEV - TAPS + 1) * FRAME :]
    halo = lax.ppermute(history, "tm", [(i, i + 1) for i in range(N_TM - 1)])
    window = jnp.asarray(window_table())
    in_vmem = pl.BlockSpec(memory_space=pltpu.VMEM)
    late_rows = (FR_DEV - EARLY) * IN_DEV
    early_rows = EARLY * IN_DEV
    params = pltpu.CompilerParams(vmem_limit_bytes=32 * MIB)
    half = FRAME // 2
    table, sign = pl.pallas_call(
        table_kernel,
        name="channel_table",
        out_shape=[jax.ShapeDtypeStruct((2, LIVE, half), bf16), jax.ShapeDtypeStruct((LIVE, 128), bf16)],
        scratch_shapes=[pltpu.VMEM((LIVE, 128), f32)] * 4,
        compiler_params=params,
        cost_estimate=cost(4e9, 3 * MIB),
    )(channel_flags.reshape(CHANNELS // 128, 128))
    folded = pl.pallas_call(
        late_kernel,
        name="filter",
        in_specs=[in_vmem, in_vmem, pl.BlockSpec(memory_space=pl.ANY)],
        out_shape=[
            jax.ShapeDtypeStruct((late_rows, half), bf16),
            jax.ShapeDtypeStruct((late_rows, half), bf16),
            jax.ShapeDtypeStruct((late_rows, 128), bf16),
        ],
        scratch_shapes=[pltpu.VMEM((late_rows, 128), f32)],
        compiler_params=params,
        cost_estimate=cost(4e9, 7 * MIB),
    )(voltages, window, table)
    late = pl.pallas_call(
        late_spectra_kernel,
        name="late_spectra",
        in_specs=[in_vmem] * 5,
        out_specs=in_vmem,
        out_shape=jax.ShapeDtypeStruct((LIVE_DEV, OWNERS * 2 * PAIRS, 128), f32),
        compiler_params=params,
        cost_estimate=cost(4e9, 12 * MIB),
    )(table, sign, *folded)
    sent = pl.pallas_call(
        spectra_kernel,
        name="spectra",
        grid=(LIVE_DEV,),
        in_specs=[in_vmem, whole((IN_DEV, EARLY * FRAME)), in_vmem, in_vmem, in_vmem, in_vmem],
        out_specs=pl.BlockSpec((OWNERS, 2 * PAIRS, 128), lambda c: (0, c, 0)),
        out_shape=pltpu.HBM((OWNERS, LIVE_DEV * 2 * PAIRS, 128), bf16),
        scratch_shapes=[
            pltpu.VMEM((early_rows, half), bf16),
            pltpu.VMEM((early_rows, half), bf16),
            pltpu.VMEM((early_rows, 128), bf16),
            pltpu.VMEM((early_rows, 128), f32),
            pltpu.VMEM((OWNERS * 2 * PAIRS, 128), f32),
        ],
        compiler_params=params,
        cost_estimate=cost(2e9, 14 * MIB),
    )(halo, voltages, window, table, sign, late)
    got = lax.all_to_all(sent, ("feed", "tm"), split_axis=0, concat_axis=0, tiled=True)
    inputs = N_FEED * IN_DEV
    rows = LIVE_DEV * 256
    return pl.pallas_call(
        beam_kernel,
        name="beams_and_power",
        in_specs=[in_vmem] * 4,
        out_specs=in_vmem,
        out_shape=jax.ShapeDtypeStruct((LIVE_DEV, UPCH, CYL * NS), f32),
        scratch_shapes=[
            pltpu.VMEM((rows, inputs), bf16),
            pltpu.VMEM((2, inputs, NS), bf16),
            pltpu.VMEM((2 * CYL, rows // 2, 2 * NS), bf16),
            pltpu.VMEM((2 * CYL, rows // 2, 2 * NS), f32),
            pltpu.VMEM((2, rows, CYL * NS), bf16),
        ],
        compiler_params=pltpu.CompilerParams(vmem_limit_bytes=36 * MIB),
        cost_estimate=cost(9e9, 6 * MIB),
    )(
        got,
        jnp.broadcast_to(feed_slot[:, None], (inputs, 128)),
        jnp.asarray(position_table(), dtype=bf16),
        jnp.asarray(sub_channel_table(), dtype=bf16),
    )


def solution(mesh):
    in_specs = (P("feed", "tm"), P(), P())
    out_specs = P(("feed", "tm"), None, None)
    return jax.shard_map(local, mesh=mesh, in_specs=in_specs, out_specs=out_specs, check_vma=False)
```

```python
import math

import jax
import jax.numpy as jnp
import numpy as np
from jax import lax
from jax.experimental import pallas as pl
from jax.experimental.pallas import tpu as pltpu
from jax.sharding import PartitionSpec as P

CHANNELS = 1024
TAPS = 4
CYL = 4
NS = 256
UPCH = 16
FRAME = 2048
N_FEED = 32
N_TM = 8
IN_DEV = 64
FR_DEV = 16
LIVE_DEV = 3
LIVE = 768
OWNERS = 256
PAIRS = FR_DEV // 2
EARLY = 4
MIB = 1 << 20


def window_table():
    length = TAPS * FRAME
    sample = np.arange(length, dtype=np.float64)
    offset = (sample - length / 2 + 0.5) / FRAME
    taper = 0.5 - 0.5 * np.cos(2.0 * np.pi * (sample + 0.5) / length)
    return (np.sinc(offset) * taper).reshape(TAPS, FRAME).astype(np.float32)


def cos_sin(modulus, first, second):
    product = np.arange(first)[:, None] * np.arange(second)[None, :] % modulus
    angle = product * (2.0 * np.pi / modulus)
    scale = 1.0 / math.sqrt(modulus)
    return np.cos(angle) * scale, np.sin(angle) * scale


def position_table():
    cosine, sine = cos_sin(NS, NS, NS)
    return np.block([[cosine, -sine], [sine, cosine]])


def sub_channel_table():
    cosine, sine = cos_sin(UPCH, UPCH, UPCH)
    real = np.stack([cosine, sine])
    imag = np.stack([-sine, cosine])
    both = np.stack([real, imag]).reshape(2, 2, PAIRS, 2, UPCH)
    return np.einsum("qrghk,bd->qbkdhrg", both, np.eye(N_TM)).reshape(256, 256)


def unit_circle(phase):
    quadrant = (phase + 256) >> 9
    x = (phase - (quadrant << 9)).astype(jnp.float32) * np.float32(2.0 * np.pi / FRAME)
    x2 = x * x
    c = 1.0 + x2 * (-0.5 + x2 * (1.0 / 24 + x2 * (-1.0 / 720 + x2 * (1.0 / 40320))))
    s = x * (1.0 + x2 * (-1.0 / 6 + x2 * (1.0 / 120 + x2 * (-1.0 / 5040 + x2 * (1.0 / 362880)))))
    odd = (quadrant & 1) == 1
    cos_mag = jnp.where(odd, s, c)
    sin_mag = jnp.where(odd, c, s)
    cosine = jnp.where(((quadrant + 1) & 2) == 2, -cos_mag, cos_mag)
    sine = jnp.where((quadrant & 2) == 2, -sin_mag, sin_mag)
    return cosine, sine


def fold_frames(window_ref, load, frames, even_ref, odd_ref, middle_ref, last_ref):
    lane = lax.broadcasted_iota(jnp.int32, (16, 128), 1)
    back = (128 - lane) & 127
    swap = lax.axis_index("feed") & 1
    last_ref[...] = jnp.zeros_like(last_ref)

    def piece(v, carry):
        sides = [pl.multiple_of(v * 128, 128), pl.multiple_of((FRAME // 128 - 1 - v) * 128, 128)]
        taps = [[window_ref[pl.ds(t, 1), pl.ds(side, 128)] for t in range(TAPS)] for side in sides]
        for rows in range(0, IN_DEV, 16):
            held = [{}, {}]
            for n, f in enumerate(frames):
                total = [None, None]
                for j in range(2):
                    for t in range(TAPS):
                        g = f - TAPS + 1 + t
                        if g not in held[j]:
                            held[j][g] = load(g, rows, sides[j]).astype(jnp.float32)
                        term = taps[j][t] * held[j][g]
                        total[j] = term if t == 0 else total[j] + term
                at = pl.ds(pl.multiple_of((n ^ swap) * IN_DEV + rows, 16), 16)
                turned = jnp.take_along_axis(total[1], back, axis=1, mode="promise_in_bounds")
                mirror = jnp.where(lane == 0, last_ref[at, :], turned)
                last_ref[at, :] = turned
                even_ref[at, pl.ds(sides[0], 128)] = (total[0] + mirror).astype(jnp.bfloat16)
                odd_ref[at, pl.ds(sides[0], 128)] = (total[0] - mirror).astype(jnp.bfloat16)
                middle_ref[at, :] = total[1].astype(jnp.bfloat16)
        return carry

    lax.fori_loop(0, FRAME // 256, piece, 0)


def table_kernel(flags_ref, table_ref, sign_ref, below_ref, channel_ref):
    lane = lax.broadcasted_iota(jnp.int32, (64, 128), 1)
    upto = (lax.broadcasted_iota(jnp.int32, (128, 128), 0) <= lax.broadcasted_iota(jnp.int32, (128, 128), 1)).astype(
        jnp.float32
    )
    ones = jnp.ones((128, 128), jnp.float32)
    sums = jnp.concatenate([upto, ones], axis=1).astype(jnp.bfloat16)
    ones = ones.astype(jnp.bfloat16)
    flags = flags_ref[...].astype(jnp.float32)
    flags = jnp.concatenate([flags, jnp.zeros_like(flags)], axis=0).astype(jnp.bfloat16)
    count = jnp.dot(flags, sums, preferred_element_type=jnp.float32)
    earlier = jnp.zeros((1, 128), jnp.float32)
    counts = []
    for r in range(CHANNELS // 128):
        counts.append((count[r : r + 1, :128] + earlier).astype(jnp.int32))
        earlier = earlier + count[r : r + 1, 128:]

    def ranks(step, carry):
        row = lax.broadcasted_iota(jnp.int32, (64, 128), 0) + step * 64
        rank = (row & (OWNERS - 1)) * LIVE_DEV + (row >> 8)
        at = pl.ds(pl.multiple_of(step * 64, 64), 64)
        below_ref[at, :] = sum((c <= rank).astype(jnp.float32) for c in counts).astype(jnp.bfloat16)
        return carry

    lax.fori_loop(0, LIVE // 64, ranks, 0)
    channel_ref[...] = jnp.dot(below_ref[...], ones, preferred_element_type=jnp.float32)

    def turn(step, carry):
        at = pl.ds(pl.multiple_of(step * 64, 64), 64)
        channel = channel_ref[at, :].astype(jnp.int32)
        scale = np.float32(1.0 / math.sqrt(FRAME))
        c, s = unit_circle((channel * lane) & (FRAME - 1))
        c, s = c * scale, s * scale
        dc, ds = unit_circle((channel * 128) & (FRAME - 1))
        sign = (1 - 2 * (channel & 1)).astype(jnp.float32) * scale
        sign_ref[at, :] = jnp.where(lane == 0, sign, 0.0).astype(jnp.bfloat16)
        for v in range(FRAME // 256):
            table_ref[0, at, v * 128 : (v + 1) * 128] = c.astype(jnp.bfloat16)
            table_ref[1, at, v * 128 : (v + 1) * 128] = (-s).astype(jnp.bfloat16)
            if v < FRAME // 256 - 1:
                c, s = dc * c - ds * s, ds * c + dc * s
        return carry

    lax.fori_loop(0, LIVE // 64, turn, 0)


def late_kernel(volt_ref, window_ref, _, even_ref, odd_ref, middle_ref, last_ref):
    def load(f, rows, lane):
        return volt_ref[rows : rows + 16, pl.ds(pl.multiple_of(f * FRAME + lane, 128), 128)]

    fold_frames(window_ref, load, range(EARLY, FR_DEV), even_ref, odd_ref, middle_ref, last_ref)


def transposed_dot(a, b):
    return lax.dot_general(a, b, (((1,), (1,)), ((), ())), preferred_element_type=jnp.float32)


def put_spectra(table, sign, even, odd, middle, wide_ref, first):
    real = transposed_dot(table[0], even) + transposed_dot(sign, middle)
    for r, value in enumerate((real, transposed_dot(table[1], odd))):
        for h in range(2):
            wide_ref[pl.ds(r * PAIRS + first + h, OWNERS, 2 * PAIRS), :] = value[:, h * 128 : (h + 1) * 128]


def late_spectra_kernel(table_ref, sign_ref, even_ref, odd_ref, middle_ref, wide_ref):
    for c in range(LIVE_DEV):
        at = slice(c * OWNERS, (c + 1) * OWNERS)
        for n in range(PAIRS // 2 - 1):
            rows = slice(n * 256, (n + 1) * 256)
            table = table_ref[0, at, :], table_ref[1, at, :]
            sources = even_ref[rows, :], odd_ref[rows, :], middle_ref[rows, :]
            put_spectra(table, sign_ref[at, :], *sources, wide_ref.at[c], 2 * (n + 1))


def spectra_kernel(
    halo_ref, volt_ref, window_ref, table_ref, sign_ref, late_ref, out_ref, even_ref, odd_ref, middle_ref, last_ref, wide_ref
):
    c = pl.program_id(0)

    @pl.when(c == 0)
    def _():
        def load(f, rows, lane):
            ref, g = (halo_ref, f + TAPS - 1) if f < 0 else (volt_ref, f)
            return ref[rows : rows + 16, pl.ds(pl.multiple_of(g * FRAME + lane, 128), 128)]

        fold_frames(window_ref, load, range(EARLY), even_ref, odd_ref, middle_ref, last_ref)

    at = pl.ds(pl.multiple_of(c * OWNERS, OWNERS), OWNERS)
    table = table_ref[0, at, :], table_ref[1, at, :]
    put_spectra(table, sign_ref[at, :], even_ref[...], odd_ref[...], middle_ref[...], wide_ref, 0)

    def join(step, carry):
        rows = pl.ds(pl.multiple_of(step * 256, 256), 256)
        early = lax.broadcasted_iota(jnp.int32, (256, 128), 0) & (PAIRS - 1) < EARLY // 2
        value = jnp.where(early, wide_ref[rows, :], late_ref[c, rows, :])
        owners = pl.ds(pl.multiple_of(step * 16, 16), 16)
        out_ref[owners] = value.reshape(16, 2 * PAIRS, 128).astype(jnp.bfloat16)
        return carry

    lax.fori_loop(0, OWNERS // 16, join, 0)


def beam_kernel(recv_ref, slot_ref, position_ref, sub_ref, out_ref, x_ref, place_ref, cell_ref, part_ref, beam_ref):
    low = lax.broadcasted_iota(jnp.int32, (2 * PAIRS, 128), 1) < IN_DEV
    groups = 2 * CYL

    def pairs(s, carry):
        lane = pl.multiple_of(s * 128, 128)
        for c in range(LIVE_DEV):
            for b in range(N_TM):
                part = slice(c * 2 * PAIRS, (c + 1) * 2 * PAIRS)
                one = recv_ref[2 * s * N_TM + b, part].astype(jnp.float32)
                two = recv_ref[(2 * s + 1) * N_TM + b, part].astype(jnp.float32)
                even = jnp.where(low, one, two)
                odd = pltpu.roll(jnp.where(low, two, one), 64, 1)
                row = c * 256 + b * 32
                x_ref[row : row + 16, pl.ds(lane, 128)] = even.astype(jnp.bfloat16)
                x_ref[row + 16 : row + 32, pl.ds(lane, 128)] = odd.astype(jnp.bfloat16)
        return carry

    lax.fori_loop(0, N_FEED // 2, pairs, 0)
    slot = jnp.concatenate([slot_ref[...]] * 2, axis=1)
    for i in range(groups):
        want = lax.broadcasted_iota(jnp.int32, slot.shape, 1) + i * NS
        place_ref[i % 2] = (slot == want).astype(jnp.float32).astype(jnp.bfloat16)
        cells = jnp.dot(x_ref[...], place_ref[i % 2], preferred_element_type=jnp.float32)
        cells = cells.reshape(-1, 2, PAIRS, NS)
        both = [cells[:, r].reshape(-1, NS) for r in range(2)]
        cell_ref[i] = jnp.concatenate(both, axis=1).astype(jnp.bfloat16)
    for p in range(2):
        for i in range(p * CYL, (p + 1) * CYL):
            part_ref[i] = jnp.dot(cell_ref[i], position_ref[...], preferred_element_type=jnp.float32)
        for f in range(LIVE_DEV * 16):
            rows = slice(f * PAIRS, (f + 1) * PAIRS)
            re = [part_ref[p * CYL + y, rows, :NS] for y in range(CYL)]
            im = [part_ref[p * CYL + y, rows, NS:] for y in range(CYL)]
            re_s, re_d = re[0] + re[2], re[0] - re[2]
            im_s, im_d = im[0] + im[2], im[0] - im[2]
            re_t, re_e = re[1] + re[3], re[1] - re[3]
            im_t, im_e = im[1] + im[3], im[1] - im[3]
            out_re = [re_s + re_t, re_d + im_e, re_s - re_t, re_d - im_e]
            out_im = [im_s + im_t, im_d - re_e, im_s - im_t, im_d + re_e]
            at = slice(f * 2 * PAIRS, (f + 1) * 2 * PAIRS)
            for e in range(CYL):
                value = jnp.concatenate([out_re[e], out_im[e]], axis=0) * 0.5
                beam_ref[p, at, e * NS : (e + 1) * NS] = value.astype(jnp.bfloat16)
    for c in range(LIVE_DEV):
        for e in range(CYL):
            total = None
            for p in range(2):
                beams = beam_ref[p, c * 256 : (c + 1) * 256, e * NS : (e + 1) * NS]
                up = jnp.dot(sub_ref[...], beams, preferred_element_type=jnp.float32)
                power = jnp.sum((up * up).reshape(2 * N_TM, UPCH, NS), axis=0)
                total = power if p == 0 else total + power
            out_ref[c, :, e * NS : (e + 1) * NS] = total * (1.0 / (2.0 * N_TM * (FR_DEV // UPCH)))


def cost(flops, nbytes):
    return pl.CostEstimate(flops=int(flops), bytes_accessed=int(nbytes), transcendentals=0)


def whole(shape, *index):
    index = index or (0,) * len(shape)
    return pl.BlockSpec(shape, lambda *_: index)


def local(voltages, feed_slot, channel_flags):
    bf16, f32 = jnp.bfloat16, jnp.float32
    history = voltages[:, (FR_DEV - TAPS + 1) * FRAME :]
    halo = lax.ppermute(history, "tm", [(i, i + 1) for i in range(N_TM - 1)])
    window = jnp.asarray(window_table())
    in_vmem = pl.BlockSpec(memory_space=pltpu.VMEM)
    late_rows = (FR_DEV - EARLY) * IN_DEV
    early_rows = EARLY * IN_DEV
    params = pltpu.CompilerParams(vmem_limit_bytes=32 * MIB)
    half = FRAME // 2
    table, sign = pl.pallas_call(
        table_kernel,
        name="channel_table",
        out_shape=[jax.ShapeDtypeStruct((2, LIVE, half), bf16), jax.ShapeDtypeStruct((LIVE, 128), bf16)],
        scratch_shapes=[pltpu.VMEM((LIVE, 128), bf16), pltpu.VMEM((LIVE, 128), f32)],
        compiler_params=params,
        cost_estimate=cost(4e9, 3 * MIB),
    )(channel_flags.reshape(CHANNELS // 128, 128))
    folded = pl.pallas_call(
        late_kernel,
        name="filter",
        in_specs=[in_vmem, in_vmem, pl.BlockSpec(memory_space=pl.ANY)],
        out_shape=[
            jax.ShapeDtypeStruct((late_rows, half), bf16),
            jax.ShapeDtypeStruct((late_rows, half), bf16),
            jax.ShapeDtypeStruct((late_rows, 128), bf16),
        ],
        scratch_shapes=[pltpu.VMEM((late_rows, 128), f32)],
        compiler_params=params,
        cost_estimate=cost(4e9, 7 * MIB),
    )(voltages, window, table)
    late = pl.pallas_call(
        late_spectra_kernel,
        name="late_spectra",
        in_specs=[in_vmem] * 5,
        out_specs=in_vmem,
        out_shape=jax.ShapeDtypeStruct((LIVE_DEV, OWNERS * 2 * PAIRS, 128), f32),
        compiler_params=params,
        cost_estimate=cost(4e9, 12 * MIB),
    )(table, sign, *folded)
    sent = pl.pallas_call(
        spectra_kernel,
        name="spectra",
        grid=(LIVE_DEV,),
        in_specs=[in_vmem] * 6,
        out_specs=pl.BlockSpec((OWNERS, 2 * PAIRS, 128), lambda c: (0, c, 0)),
        out_shape=pltpu.HBM((OWNERS, LIVE_DEV * 2 * PAIRS, 128), bf16),
        scratch_shapes=[
            pltpu.VMEM((early_rows, half), bf16),
            pltpu.VMEM((early_rows, half), bf16),
            pltpu.VMEM((early_rows, 128), bf16),
            pltpu.VMEM((early_rows, 128), f32),
            pltpu.VMEM((OWNERS * 2 * PAIRS, 128), f32),
        ],
        compiler_params=params,
        cost_estimate=cost(2e9, 14 * MIB),
    )(halo, voltages, window, table, sign, late)
    got = lax.all_to_all(sent, ("feed", "tm"), split_axis=0, concat_axis=0, tiled=True)
    inputs = N_FEED * IN_DEV
    rows = LIVE_DEV * 256
    return pl.pallas_call(
        beam_kernel,
        name="beams_and_power",
        in_specs=[in_vmem] * 4,
        out_specs=in_vmem,
        out_shape=jax.ShapeDtypeStruct((LIVE_DEV, UPCH, CYL * NS), f32),
        scratch_shapes=[
            pltpu.VMEM((rows, inputs), bf16),
            pltpu.VMEM((2, inputs, NS), bf16),
            pltpu.VMEM((2 * CYL, rows // 2, 2 * NS), bf16),
            pltpu.VMEM((2 * CYL, rows // 2, 2 * NS), f32),
            pltpu.VMEM((2, rows, CYL * NS), bf16),
        ],
        compiler_params=pltpu.CompilerParams(vmem_limit_bytes=36 * MIB),
        cost_estimate=cost(9e9, 6 * MIB),
    )(
        got,
        jnp.broadcast_to(feed_slot[:, None], (inputs, 128)),
        jnp.asarray(position_table(), dtype=bf16),
        jnp.asarray(sub_channel_table(), dtype=bf16),
    )


def solution(mesh):
    in_specs = (P("feed", "tm"), P(), P())
    out_specs = P(("feed", "tm"), None, None)
    return jax.shard_map(local, mesh=mesh, in_specs=in_specs, out_specs=out_specs, check_vma=False)
```

```python
import math

import jax
import jax.numpy as jnp
import numpy as np
from jax import lax
from jax.experimental import pallas as pl
from jax.experimental.pallas import tpu as pltpu
from jax.sharding import PartitionSpec as P

CHANNELS = 1024
TAPS = 4
CYL = 4
NS = 256
UPCH = 16
FRAME = 2048
N_FEED = 32
N_TM = 8
IN_DEV = 64
FR_DEV = 16
LIVE_DEV = 3
LIVE = 768
OWNERS = 256
OWNER_BLOCK = 64
PAIRS = FR_DEV // 2
EARLY = 4
MIB = 1 << 20


def window_table():
    length = TAPS * FRAME
    sample = np.arange(length, dtype=np.float64)
    offset = (sample - length / 2 + 0.5) / FRAME
    taper = 0.5 - 0.5 * np.cos(2.0 * np.pi * (sample + 0.5) / length)
    return (np.sinc(offset) * taper).reshape(TAPS, FRAME).astype(np.float32)


def cos_sin(modulus, first, second):
    product = np.arange(first)[:, None] * np.arange(second)[None, :] % modulus
    angle = product * (2.0 * np.pi / modulus)
    scale = 1.0 / math.sqrt(modulus)
    return np.cos(angle) * scale, np.sin(angle) * scale


def position_table():
    cosine, sine = cos_sin(NS, NS, NS)
    return np.block([[cosine, -sine], [sine, cosine]])


def sub_channel_table():
    cosine, sine = cos_sin(UPCH, UPCH, UPCH)
    real = np.stack([cosine, sine])
    imag = np.stack([-sine, cosine])
    both = np.stack([real, imag]).reshape(2, 2, PAIRS, 2, UPCH)
    return np.einsum("qrghk,bd->qbkdhrg", both, np.eye(N_TM)).reshape(256, 256)


def unit_circle(phase):
    quadrant = (phase + 256) >> 9
    x = (phase - (quadrant << 9)).astype(jnp.float32) * np.float32(2.0 * np.pi / FRAME)
    x2 = x * x
    c = 1.0 + x2 * (-0.5 + x2 * (1.0 / 24 + x2 * (-1.0 / 720 + x2 * (1.0 / 40320))))
    s = x * (1.0 + x2 * (-1.0 / 6 + x2 * (1.0 / 120 + x2 * (-1.0 / 5040 + x2 * (1.0 / 362880)))))
    odd = (quadrant & 1) == 1
    cos_mag = jnp.where(odd, s, c)
    sin_mag = jnp.where(odd, c, s)
    cosine = jnp.where(((quadrant + 1) & 2) == 2, -cos_mag, cos_mag)
    sine = jnp.where((quadrant & 2) == 2, -sin_mag, sin_mag)
    return cosine, sine


def fold_frames(*args):
    odd = lax.axis_index("feed") & 1
    for swap in range(2):

        @pl.when(odd == swap)
        def _():
            fold_placed(swap, *args)


def fold_placed(swap, window_ref, load, frames, even_ref, odd_ref, middle_ref, last_ref):
    lane = lax.broadcasted_iota(jnp.int32, (16, 128), 1)
    back = (128 - lane) & 127
    last_ref[...] = jnp.zeros_like(last_ref)

    def piece(v, carry):
        sides = [pl.multiple_of(v * 128, 128), pl.multiple_of((FRAME // 128 - 1 - v) * 128, 128)]
        taps = [[window_ref[pl.ds(t, 1), pl.ds(side, 128)] for t in range(TAPS)] for side in sides]
        for rows in range(0, IN_DEV, 16):
            held = [{}, {}]
            for n, f in enumerate(frames):
                total = [None, None]
                for j in range(2):
                    for t in range(TAPS):
                        g = f - TAPS + 1 + t
                        if g not in held[j]:
                            held[j][g] = load(g, rows, sides[j]).astype(jnp.float32)
                        term = taps[j][t] * held[j][g]
                        total[j] = term if t == 0 else total[j] + term
                at = slice((n ^ swap) * IN_DEV + rows, (n ^ swap) * IN_DEV + rows + 16)
                turned = jnp.take_along_axis(total[1], back, axis=1, mode="promise_in_bounds")
                mirror = jnp.where(lane == 0, last_ref[at, :], turned)
                last_ref[at, :] = turned
                even_ref[at, pl.ds(sides[0], 128)] = (total[0] + mirror).astype(jnp.bfloat16)
                odd_ref[at, pl.ds(sides[0], 128)] = (total[0] - mirror).astype(jnp.bfloat16)
                middle_ref[at, :] = total[1].astype(jnp.bfloat16)
        return carry

    lax.fori_loop(0, FRAME // 256, piece, 0)


def table_kernel(flags_ref, table_ref, sign_ref, below_ref, channel_ref):
    lane = lax.broadcasted_iota(jnp.int32, (64, 128), 1)
    upto = (lax.broadcasted_iota(jnp.int32, (128, 128), 0) <= lax.broadcasted_iota(jnp.int32, (128, 128), 1)).astype(
        jnp.float32
    )
    ones = jnp.ones((128, 128), jnp.float32)
    sums = jnp.concatenate([upto, ones], axis=1).astype(jnp.bfloat16)
    ones = ones.astype(jnp.bfloat16)
    flags = flags_ref[...].astype(jnp.float32)
    flags = jnp.concatenate([flags, jnp.zeros_like(flags)], axis=0).astype(jnp.bfloat16)
    count = jnp.dot(flags, sums, preferred_element_type=jnp.float32)
    earlier = jnp.zeros((1, 128), jnp.float32)
    counts = []
    for r in range(CHANNELS // 128):
        counts.append((count[r : r + 1, :128] + earlier).astype(jnp.int32))
        earlier = earlier + count[r : r + 1, 128:]

    def ranks(step, carry):
        row = lax.broadcasted_iota(jnp.int32, (64, 128), 0) + step * 64
        rank = (row & (OWNERS - 1)) * LIVE_DEV + (row >> 8)
        at = pl.ds(pl.multiple_of(step * 64, 64), 64)
        below_ref[at, :] = sum((c <= rank).astype(jnp.float32) for c in counts).astype(jnp.bfloat16)
        return carry

    lax.fori_loop(0, LIVE // 64, ranks, 0)
    channel_ref[...] = jnp.dot(below_ref[...], ones, preferred_element_type=jnp.float32)

    def turn(step, carry):
        at = pl.ds(pl.multiple_of(step * 64, 64), 64)
        channel = channel_ref[at, :].astype(jnp.int32)
        scale = np.float32(1.0 / math.sqrt(FRAME))
        c, s = unit_circle((channel * lane) & (FRAME - 1))
        c, s = c * scale, s * scale
        dc, ds = unit_circle((channel * 128) & (FRAME - 1))
        sign = (1 - 2 * (channel & 1)).astype(jnp.float32) * scale
        sign_ref[at, :] = jnp.where(lane == 0, sign, 0.0).astype(jnp.bfloat16)
        for v in range(FRAME // 256):
            table_ref[0, at, v * 128 : (v + 1) * 128] = c.astype(jnp.bfloat16)
            table_ref[1, at, v * 128 : (v + 1) * 128] = (-s).astype(jnp.bfloat16)
            if v < FRAME // 256 - 1:
                c, s = dc * c - ds * s, ds * c + dc * s
        return carry

    lax.fori_loop(0, LIVE // 64, turn, 0)


def late_kernel(volt_ref, window_ref, _, even_ref, odd_ref, middle_ref, last_ref):
    def load(f, rows, lane):
        return volt_ref[rows : rows + 16, pl.ds(pl.multiple_of(f * FRAME + lane, 128), 128)]

    fold_frames(window_ref, load, range(EARLY, FR_DEV), even_ref, odd_ref, middle_ref, last_ref)


def transposed_dot(a, b):
    return lax.dot_general(a, b, (((1,), (1,)), ((), ())), preferred_element_type=jnp.float32)


def put_spectra(table_ref, sign_ref, even, odd, middle, wide_ref, first):
    real = transposed_dot(table_ref[0], even) + transposed_dot(sign_ref[...], middle)
    for r, value in enumerate((real, transposed_dot(table_ref[1], odd))):
        for c in range(LIVE_DEV):
            for h in range(2):
                part = value[c * OWNERS : (c + 1) * OWNERS, h * 128 : (h + 1) * 128]
                wide_ref[c, pl.ds(r * PAIRS + first + h, OWNERS, 2 * PAIRS), :] = part


def late_spectra_kernel(table_ref, sign_ref, even_ref, odd_ref, middle_ref, wide_ref):
    for n in range(PAIRS // 2 - 1):
        rows = slice(n * 256, (n + 1) * 256)
        put_spectra(table_ref, sign_ref, even_ref[rows, :], odd_ref[rows, :], middle_ref[rows, :], wide_ref, 2 * (n + 1))


def spectra_kernel(
    halo_ref, volt_ref, window_ref, table_ref, sign_ref, late_ref, out_ref, even_ref, odd_ref, middle_ref, last_ref, wide_ref
):
    step = pl.program_id(0)

    @pl.when(step == 0)
    def _():
        def load(f, rows, lane):
            ref, g = (halo_ref, f + TAPS - 1) if f < 0 else (volt_ref, f)
            return ref[rows : rows + 16, pl.ds(pl.multiple_of(g * FRAME + lane, 128), 128)]

        fold_frames(window_ref, load, range(EARLY), even_ref, odd_ref, middle_ref, last_ref)
        put_spectra(table_ref, sign_ref, even_ref[...], odd_ref[...], middle_ref[...], wide_ref, 0)

    size = OWNER_BLOCK * 2 * PAIRS
    early = lax.broadcasted_iota(jnp.int32, (size, 128), 0) & (PAIRS - 1) < EARLY // 2
    rows = pl.ds(pl.multiple_of(step * size, size), size)
    for c in range(LIVE_DEV):
        value = jnp.where(early, wide_ref[c, rows, :], late_ref[c, rows, :])
        part = slice(c * 2 * PAIRS, (c + 1) * 2 * PAIRS)
        out_ref[:, part, :] = value.reshape(OWNER_BLOCK, 2 * PAIRS, 128).astype(jnp.bfloat16)


def beam_kernel(recv_ref, slot_ref, position_ref, sub_ref, out_ref, x_ref, place_ref, cell_ref, part_ref, beam_ref):
    low = lax.broadcasted_iota(jnp.int32, (2 * PAIRS, 128), 1) < IN_DEV
    groups = 2 * CYL

    def pairs(s, carry):
        lane = pl.multiple_of(s * 128, 128)
        for c in range(LIVE_DEV):
            for b in range(N_TM):
                part = slice(c * 2 * PAIRS, (c + 1) * 2 * PAIRS)
                one = recv_ref[2 * s * N_TM + b, part].astype(jnp.float32)
                two = recv_ref[(2 * s + 1) * N_TM + b, part].astype(jnp.float32)
                even = jnp.where(low, one, two)
                odd = pltpu.roll(jnp.where(low, two, one), 64, 1)
                row = c * 256 + b * 32
                x_ref[row : row + 16, pl.ds(lane, 128)] = even.astype(jnp.bfloat16)
                x_ref[row + 16 : row + 32, pl.ds(lane, 128)] = odd.astype(jnp.bfloat16)
        return carry

    lax.fori_loop(0, N_FEED // 2, pairs, 0)
    slot = jnp.concatenate([slot_ref[...]] * 2, axis=1)
    for i in range(groups):
        want = lax.broadcasted_iota(jnp.int32, slot.shape, 1) + i * NS
        place_ref[i % 2] = (slot == want).astype(jnp.float32).astype(jnp.bfloat16)
        cells = jnp.dot(x_ref[...], place_ref[i % 2], preferred_element_type=jnp.float32)
        cells = cells.reshape(-1, 2, PAIRS, NS)
        both = [cells[:, r].reshape(-1, NS) for r in range(2)]
        cell_ref[i] = jnp.concatenate(both, axis=1).astype(jnp.bfloat16)
    for p in range(2):
        for i in range(p * CYL, (p + 1) * CYL):
            part_ref[i] = jnp.dot(cell_ref[i], position_ref[...], preferred_element_type=jnp.float32)
        for f in range(LIVE_DEV * 16):
            rows = slice(f * PAIRS, (f + 1) * PAIRS)
            re = [part_ref[p * CYL + y, rows, :NS] for y in range(CYL)]
            im = [part_ref[p * CYL + y, rows, NS:] for y in range(CYL)]
            re_s, re_d = re[0] + re[2], re[0] - re[2]
            im_s, im_d = im[0] + im[2], im[0] - im[2]
            re_t, re_e = re[1] + re[3], re[1] - re[3]
            im_t, im_e = im[1] + im[3], im[1] - im[3]
            out_re = [re_s + re_t, re_d + im_e, re_s - re_t, re_d - im_e]
            out_im = [im_s + im_t, im_d - re_e, im_s - im_t, im_d + re_e]
            at = slice(f * 2 * PAIRS, (f + 1) * 2 * PAIRS)
            for e in range(CYL):
                value = jnp.concatenate([out_re[e], out_im[e]], axis=0) * 0.5
                beam_ref[p, at, e * NS : (e + 1) * NS] = value.astype(jnp.bfloat16)
    for c in range(LIVE_DEV):
        for e in range(CYL):
            total = None
            for p in range(2):
                beams = beam_ref[p, c * 256 : (c + 1) * 256, e * NS : (e + 1) * NS]
                up = jnp.dot(sub_ref[...], beams, preferred_element_type=jnp.float32)
                power = jnp.sum((up * up).reshape(2 * N_TM, UPCH, NS), axis=0)
                total = power if p == 0 else total + power
            out_ref[c, :, e * NS : (e + 1) * NS] = total * (1.0 / (2.0 * N_TM * (FR_DEV // UPCH)))


def cost(flops, nbytes):
    return pl.CostEstimate(flops=int(flops), bytes_accessed=int(nbytes), transcendentals=0)


def local(voltages, feed_slot, channel_flags):
    bf16, f32 = jnp.bfloat16, jnp.float32
    history = voltages[:, (FR_DEV - TAPS + 1) * FRAME :]
    halo = lax.ppermute(history, "tm", [(i, i + 1) for i in range(N_TM - 1)])
    window = jnp.asarray(window_table())
    in_vmem = pl.BlockSpec(memory_space=pltpu.VMEM)
    late_rows = (FR_DEV - EARLY) * IN_DEV
    early_rows = EARLY * IN_DEV
    params = pltpu.CompilerParams(vmem_limit_bytes=32 * MIB)
    half = FRAME // 2
    table, sign = pl.pallas_call(
        table_kernel,
        name="channel_table",
        out_shape=[jax.ShapeDtypeStruct((2, LIVE, half), bf16), jax.ShapeDtypeStruct((LIVE, 128), bf16)],
        scratch_shapes=[pltpu.VMEM((LIVE, 128), bf16), pltpu.VMEM((LIVE, 128), f32)],
        compiler_params=params,
        cost_estimate=cost(4e9, 3 * MIB),
    )(channel_flags.reshape(CHANNELS // 128, 128))
    folded = pl.pallas_call(
        late_kernel,
        name="filter",
        in_specs=[in_vmem, in_vmem, pl.BlockSpec(memory_space=pl.ANY)],
        out_shape=[
            jax.ShapeDtypeStruct((late_rows, half), bf16),
            jax.ShapeDtypeStruct((late_rows, half), bf16),
            jax.ShapeDtypeStruct((late_rows, 128), bf16),
        ],
        scratch_shapes=[pltpu.VMEM((late_rows, 128), f32)],
        compiler_params=params,
        cost_estimate=cost(4e9, 7 * MIB),
    )(voltages, window, table)
    late = pl.pallas_call(
        late_spectra_kernel,
        name="late_spectra",
        in_specs=[in_vmem] * 5,
        out_specs=in_vmem,
        out_shape=jax.ShapeDtypeStruct((LIVE_DEV, OWNERS * 2 * PAIRS, 128), f32),
        compiler_params=params,
        cost_estimate=cost(4e9, 12 * MIB),
    )(table, sign, *folded)
    sent = pl.pallas_call(
        spectra_kernel,
        name="spectra",
        grid=(OWNERS // OWNER_BLOCK,),
        in_specs=[in_vmem] * 6,
        out_specs=pl.BlockSpec((OWNER_BLOCK, LIVE_DEV * 2 * PAIRS, 128), lambda step: (step, 0, 0)),
        out_shape=pltpu.HBM((OWNERS, LIVE_DEV * 2 * PAIRS, 128), bf16),
        scratch_shapes=[
            pltpu.VMEM((early_rows, half), bf16),
            pltpu.VMEM((early_rows, half), bf16),
            pltpu.VMEM((early_rows, 128), bf16),
            pltpu.VMEM((early_rows, 128), f32),
            pltpu.VMEM((LIVE_DEV, OWNERS * 2 * PAIRS, 128), f32),
        ],
        compiler_params=params,
        cost_estimate=cost(2e9, 14 * MIB),
    )(halo, voltages, window, table, sign, late)
    got = lax.all_to_all(sent, ("feed", "tm"), split_axis=0, concat_axis=0, tiled=True)
    inputs = N_FEED * IN_DEV
    rows = LIVE_DEV * 256
    return pl.pallas_call(
        beam_kernel,
        name="beams_and_power",
        in_specs=[in_vmem] * 4,
        out_specs=in_vmem,
        out_shape=jax.ShapeDtypeStruct((LIVE_DEV, UPCH, CYL * NS), f32),
        scratch_shapes=[
            pltpu.VMEM((rows, inputs), bf16),
            pltpu.VMEM((2, inputs, NS), bf16),
            pltpu.VMEM((2 * CYL, rows // 2, 2 * NS), bf16),
            pltpu.VMEM((2 * CYL, rows // 2, 2 * NS), f32),
            pltpu.VMEM((2, rows, CYL * NS), bf16),
        ],
        compiler_params=pltpu.CompilerParams(vmem_limit_bytes=36 * MIB),
        cost_estimate=cost(9e9, 6 * MIB),
    )(
        got,
        jnp.broadcast_to(feed_slot[:, None], (inputs, 128)),
        jnp.asarray(position_table(), dtype=bf16),
        jnp.asarray(sub_channel_table(), dtype=bf16),
    )


def solution(mesh):
    in_specs = (P("feed", "tm"), P(), P())
    out_specs = P(("feed", "tm"), None, None)
    return jax.shard_map(local, mesh=mesh, in_specs=in_specs, out_specs=out_specs, check_vma=False)
```

```python
import math

import jax
import jax.numpy as jnp
import numpy as np
from jax import lax
from jax.experimental import pallas as pl
from jax.experimental.pallas import tpu as pltpu
from jax.sharding import PartitionSpec as P

CHANNELS = 1024
TAPS = 4
CYL = 4
NS = 256
UPCH = 16
FRAME = 2048
N_FEED = 32
N_TM = 8
IN_DEV = 64
FR_DEV = 16
LIVE_DEV = 3
LIVE = 768
OWNERS = 256
OWNER_BLOCK = 64
PAIRS = FR_DEV // 2
EARLY = 4
MIB = 1 << 20


def window_table():
    length = TAPS * FRAME
    sample = np.arange(length, dtype=np.float64)
    offset = (sample - length / 2 + 0.5) / FRAME
    taper = 0.5 - 0.5 * np.cos(2.0 * np.pi * (sample + 0.5) / length)
    return (np.sinc(offset) * taper).reshape(TAPS, FRAME).astype(np.float32)


def cos_sin(modulus, first, second):
    product = np.arange(first)[:, None] * np.arange(second)[None, :] % modulus
    angle = product * (2.0 * np.pi / modulus)
    scale = 1.0 / math.sqrt(modulus)
    return np.cos(angle) * scale, np.sin(angle) * scale


def position_table():
    cosine, sine = cos_sin(NS, NS, NS)
    return np.block([[cosine, -sine], [sine, cosine]])


def sub_channel_table():
    cosine, sine = cos_sin(UPCH, UPCH, UPCH)
    real = np.stack([cosine, sine])
    imag = np.stack([-sine, cosine])
    both = np.stack([real, imag]).reshape(2, 2, PAIRS, 2, UPCH)
    return np.einsum("qrghk,bd->qbkdhrg", both, np.eye(N_TM)).reshape(256, 256)


def unit_circle(phase):
    quadrant = (phase + 256) >> 9
    x = (phase - (quadrant << 9)).astype(jnp.float32) * np.float32(2.0 * np.pi / FRAME)
    x2 = x * x
    c = 1.0 + x2 * (-0.5 + x2 * (1.0 / 24 + x2 * (-1.0 / 720 + x2 * (1.0 / 40320))))
    s = x * (1.0 + x2 * (-1.0 / 6 + x2 * (1.0 / 120 + x2 * (-1.0 / 5040 + x2 * (1.0 / 362880)))))
    odd = (quadrant & 1) == 1
    cos_mag = jnp.where(odd, s, c)
    sin_mag = jnp.where(odd, c, s)
    cosine = jnp.where(((quadrant + 1) & 2) == 2, -cos_mag, cos_mag)
    sine = jnp.where((quadrant & 2) == 2, -sin_mag, sin_mag)
    return cosine, sine


def fold_frames(*args):
    odd = lax.axis_index("feed") & 1
    for swap in range(2):

        @pl.when(odd == swap)
        def _():
            fold_placed(swap, *args)


def fold_placed(swap, window_ref, load, frames, even_ref, odd_ref, middle_ref, last_ref):
    lane = lax.broadcasted_iota(jnp.int32, (16, 128), 1)
    back = (128 - lane) & 127
    last_ref[...] = jnp.zeros_like(last_ref)

    def piece(v, carry):
        sides = [pl.multiple_of(v * 128, 128), pl.multiple_of((FRAME // 128 - 1 - v) * 128, 128)]
        taps = [[window_ref[pl.ds(t, 1), pl.ds(side, 128)] for t in range(TAPS)] for side in sides]
        for rows in range(0, IN_DEV, 16):
            held = [{}, {}]
            for n, f in enumerate(frames):
                total = [None, None]
                for j in range(2):
                    for t in range(TAPS):
                        g = f - TAPS + 1 + t
                        if g not in held[j]:
                            held[j][g] = load(g, rows, sides[j]).astype(jnp.float32)
                        term = taps[j][t] * held[j][g]
                        total[j] = term if t == 0 else total[j] + term
                at = slice((n ^ swap) * IN_DEV + rows, (n ^ swap) * IN_DEV + rows + 16)
                turned = jnp.take_along_axis(total[1], back, axis=1, mode="promise_in_bounds")
                mirror = jnp.where(lane == 0, last_ref[at, :], turned)
                last_ref[at, :] = turned
                even_ref[at, pl.ds(sides[0], 128)] = (total[0] + mirror).astype(jnp.bfloat16)
                odd_ref[at, pl.ds(sides[0], 128)] = (total[0] - mirror).astype(jnp.bfloat16)
                middle_ref[at, :] = total[1].astype(jnp.bfloat16)
        return carry

    lax.fori_loop(0, FRAME // 256, piece, 0)


def table_kernel(flags_ref, table_ref, sign_ref, below_ref, channel_ref):
    lane = lax.broadcasted_iota(jnp.int32, (64, 128), 1)
    upto = (lax.broadcasted_iota(jnp.int32, (128, 128), 0) <= lax.broadcasted_iota(jnp.int32, (128, 128), 1)).astype(
        jnp.float32
    )
    ones = jnp.ones((128, 128), jnp.float32)
    sums = jnp.concatenate([upto, ones], axis=1).astype(jnp.bfloat16)
    ones = ones.astype(jnp.bfloat16)
    flags = flags_ref[...].astype(jnp.float32)
    flags = jnp.concatenate([flags, jnp.zeros_like(flags)], axis=0).astype(jnp.bfloat16)
    count = jnp.dot(flags, sums, preferred_element_type=jnp.float32)
    earlier = jnp.zeros((1, 128), jnp.float32)
    counts = []
    for r in range(CHANNELS // 128):
        counts.append((count[r : r + 1, :128] + earlier).astype(jnp.int32))
        earlier = earlier + count[r : r + 1, 128:]

    def ranks(step, carry):
        row = lax.broadcasted_iota(jnp.int32, (64, 128), 0) + step * 64
        rank = (row & (OWNERS - 1)) * LIVE_DEV + (row >> 8)
        at = pl.ds(pl.multiple_of(step * 64, 64), 64)
        below_ref[at, :] = sum((c <= rank).astype(jnp.float32) for c in counts).astype(jnp.bfloat16)
        return carry

    lax.fori_loop(0, LIVE // 64, ranks, 0)
    channel_ref[...] = jnp.dot(below_ref[...], ones, preferred_element_type=jnp.float32)

    def turn(step, carry):
        at = pl.ds(pl.multiple_of(step * 64, 64), 64)
        channel = channel_ref[at, :].astype(jnp.int32)
        scale = np.float32(1.0 / math.sqrt(FRAME))
        c, s = unit_circle((channel * lane) & (FRAME - 1))
        c, s = c * scale, s * scale
        dc, ds = unit_circle((channel * 128) & (FRAME - 1))
        sign = (1 - 2 * (channel & 1)).astype(jnp.float32) * scale
        sign_ref[at, :] = jnp.where(lane == 0, sign, 0.0).astype(jnp.bfloat16)
        for v in range(FRAME // 256):
            table_ref[0, at, v * 128 : (v + 1) * 128] = c.astype(jnp.bfloat16)
            table_ref[1, at, v * 128 : (v + 1) * 128] = (-s).astype(jnp.bfloat16)
            if v < FRAME // 256 - 1:
                c, s = dc * c - ds * s, ds * c + dc * s
        return carry

    lax.fori_loop(0, LIVE // 64, turn, 0)


def late_kernel(volt_ref, window_ref, _, even_ref, odd_ref, middle_ref, last_ref):
    def load(f, rows, lane):
        return volt_ref[rows : rows + 16, pl.ds(pl.multiple_of(f * FRAME + lane, 128), 128)]

    fold_frames(window_ref, load, range(EARLY, FR_DEV), even_ref, odd_ref, middle_ref, last_ref)


def transposed_dot(a, b):
    return lax.dot_general(a, b, (((1,), (1,)), ((), ())), preferred_element_type=jnp.float32)


def put_spectra(table_ref, sign_ref, even, odd, middle, wide_ref, first):
    real = transposed_dot(table_ref[0], even) + transposed_dot(sign_ref[...], middle)
    for r, value in enumerate((real, transposed_dot(table_ref[1], odd))):
        for c in range(LIVE_DEV):
            for h in range(2):
                part = value[c * OWNERS : (c + 1) * OWNERS, h * 128 : (h + 1) * 128]
                wide_ref[c, pl.ds(r * PAIRS + first + h, OWNERS, 2 * PAIRS), :] = part


def late_spectra_kernel(table_ref, sign_ref, even_ref, odd_ref, middle_ref, wide_ref):
    for n in range(PAIRS // 2 - 1):
        rows = slice(n * 256, (n + 1) * 256)
        put_spectra(table_ref, sign_ref, even_ref[rows, :], odd_ref[rows, :], middle_ref[rows, :], wide_ref, 2 * (n + 1))


def spectra_kernel(
    halo_ref, volt_ref, window_ref, table_ref, sign_ref, late_ref, out_ref, even_ref, odd_ref, middle_ref, last_ref, wide_ref
):
    step = pl.program_id(0)

    @pl.when(step == 0)
    def _():
        def load(f, rows, lane):
            ref, g = (halo_ref, f + TAPS - 1) if f < 0 else (volt_ref, f)
            return ref[rows : rows + 16, pl.ds(pl.multiple_of(g * FRAME + lane, 128), 128)]

        fold_frames(window_ref, load, range(EARLY), even_ref, odd_ref, middle_ref, last_ref)
        put_spectra(table_ref, sign_ref, even_ref[...], odd_ref[...], middle_ref[...], wide_ref, 0)

    size = OWNER_BLOCK * 2 * PAIRS
    early = lax.broadcasted_iota(jnp.int32, (size, 128), 0) & (PAIRS - 1) < EARLY // 2
    rows = pl.ds(pl.multiple_of(step * size, size), size)
    for c in range(LIVE_DEV):
        value = jnp.where(early, wide_ref[c, rows, :], late_ref[c, rows, :])
        part = slice(c * 2 * PAIRS, (c + 1) * 2 * PAIRS)
        out_ref[:, part, :] = value.reshape(OWNER_BLOCK, 2 * PAIRS, 128).astype(jnp.bfloat16)


def beam_kernel(recv_ref, slot_ref, position_ref, sub_ref, out_ref, x_ref, place_ref, cell_ref, part_ref, beam_ref):
    low = lax.broadcasted_iota(jnp.int32, (2 * PAIRS, 128), 1) < IN_DEV
    groups = 2 * CYL

    def pairs(s, carry):
        lane = pl.multiple_of(s * 128, 128)
        for c in range(LIVE_DEV):
            for b in range(N_TM):
                part = slice(c * 2 * PAIRS, (c + 1) * 2 * PAIRS)
                one = recv_ref[2 * s * N_TM + b, part].astype(jnp.float32)
                two = recv_ref[(2 * s + 1) * N_TM + b, part].astype(jnp.float32)
                even = jnp.where(low, one, two)
                odd = pltpu.roll(jnp.where(low, two, one), 64, 1)
                row = c * 256 + b * 32
                x_ref[row : row + 16, pl.ds(lane, 128)] = even.astype(jnp.bfloat16)
                x_ref[row + 16 : row + 32, pl.ds(lane, 128)] = odd.astype(jnp.bfloat16)
        return carry

    lax.fori_loop(0, N_FEED // 2, pairs, 0)
    slot = slot_ref[...]
    for i in range(groups):
        want = lax.broadcasted_iota(jnp.int32, (NS, N_FEED * IN_DEV), 0) + i * NS
        place_ref[i % 2] = (slot == want).astype(jnp.float32).astype(jnp.bfloat16)
        cells = transposed_dot(x_ref[...], place_ref[i % 2])
        cells = cells.reshape(-1, 2, PAIRS, NS)
        both = [cells[:, r].reshape(-1, NS) for r in range(2)]
        cell_ref[i] = jnp.concatenate(both, axis=1).astype(jnp.bfloat16)
    for p in range(2):
        for i in range(p * CYL, (p + 1) * CYL):
            part_ref[i] = jnp.dot(cell_ref[i], position_ref[...], preferred_element_type=jnp.float32)
        for f in range(LIVE_DEV * 16):
            rows = slice(f * PAIRS, (f + 1) * PAIRS)
            re = [part_ref[p * CYL + y, rows, :NS] for y in range(CYL)]
            im = [part_ref[p * CYL + y, rows, NS:] for y in range(CYL)]
            re_s, re_d = re[0] + re[2], re[0] - re[2]
            im_s, im_d = im[0] + im[2], im[0] - im[2]
            re_t, re_e = re[1] + re[3], re[1] - re[3]
            im_t, im_e = im[1] + im[3], im[1] - im[3]
            out_re = [re_s + re_t, re_d + im_e, re_s - re_t, re_d - im_e]
            out_im = [im_s + im_t, im_d - re_e, im_s - im_t, im_d + re_e]
            at = slice(f * 2 * PAIRS, (f + 1) * 2 * PAIRS)
            for e in range(CYL):
                value = jnp.concatenate([out_re[e], out_im[e]], axis=0) * 0.5
                beam_ref[p, at, e * NS : (e + 1) * NS] = value.astype(jnp.bfloat16)
    for c in range(LIVE_DEV):
        for e in range(CYL):
            total = None
            for p in range(2):
                beams = beam_ref[p, c * 256 : (c + 1) * 256, e * NS : (e + 1) * NS]
                up = jnp.dot(sub_ref[...], beams, preferred_element_type=jnp.float32)
                power = jnp.sum((up * up).reshape(2 * N_TM, UPCH, NS), axis=0)
                total = power if p == 0 else total + power
            out_ref[c, :, e * NS : (e + 1) * NS] = total * (1.0 / (2.0 * N_TM * (FR_DEV // UPCH)))


def cost(flops, nbytes):
    return pl.CostEstimate(flops=int(flops), bytes_accessed=int(nbytes), transcendentals=0)


def local(voltages, feed_slot, channel_flags):
    bf16, f32 = jnp.bfloat16, jnp.float32
    history = voltages[:, (FR_DEV - TAPS + 1) * FRAME :]
    halo = lax.ppermute(history, "tm", [(i, i + 1) for i in range(N_TM - 1)])
    window = jnp.asarray(window_table())
    in_vmem = pl.BlockSpec(memory_space=pltpu.VMEM)
    late_rows = (FR_DEV - EARLY) * IN_DEV
    early_rows = EARLY * IN_DEV
    params = pltpu.CompilerParams(vmem_limit_bytes=32 * MIB)
    half = FRAME // 2
    table, sign = pl.pallas_call(
        table_kernel,
        name="channel_table",
        out_shape=[jax.ShapeDtypeStruct((2, LIVE, half), bf16), jax.ShapeDtypeStruct((LIVE, 128), bf16)],
        scratch_shapes=[pltpu.VMEM((LIVE, 128), bf16), pltpu.VMEM((LIVE, 128), f32)],
        compiler_params=params,
        cost_estimate=cost(4e9, 3 * MIB),
    )(channel_flags.reshape(CHANNELS // 128, 128))
    folded = pl.pallas_call(
        late_kernel,
        name="filter",
        in_specs=[in_vmem, in_vmem, pl.BlockSpec(memory_space=pl.ANY)],
        out_shape=[
            jax.ShapeDtypeStruct((late_rows, half), bf16),
            jax.ShapeDtypeStruct((late_rows, half), bf16),
            jax.ShapeDtypeStruct((late_rows, 128), bf16),
        ],
        scratch_shapes=[pltpu.VMEM((late_rows, 128), f32)],
        compiler_params=params,
        cost_estimate=cost(4e9, 7 * MIB),
    )(voltages, window, table)
    late = pl.pallas_call(
        late_spectra_kernel,
        name="late_spectra",
        in_specs=[in_vmem] * 5,
        out_specs=in_vmem,
        out_shape=jax.ShapeDtypeStruct((LIVE_DEV, OWNERS * 2 * PAIRS, 128), f32),
        compiler_params=params,
        cost_estimate=cost(4e9, 12 * MIB),
    )(table, sign, *folded)
    sent = pl.pallas_call(
        spectra_kernel,
        name="spectra",
        grid=(OWNERS // OWNER_BLOCK,),
        in_specs=[in_vmem] * 6,
        out_specs=pl.BlockSpec((OWNER_BLOCK, LIVE_DEV * 2 * PAIRS, 128), lambda step: (step, 0, 0)),
        out_shape=pltpu.HBM((OWNERS, LIVE_DEV * 2 * PAIRS, 128), bf16),
        scratch_shapes=[
            pltpu.VMEM((early_rows, half), bf16),
            pltpu.VMEM((early_rows, half), bf16),
            pltpu.VMEM((early_rows, 128), bf16),
            pltpu.VMEM((early_rows, 128), f32),
            pltpu.VMEM((LIVE_DEV, OWNERS * 2 * PAIRS, 128), f32),
        ],
        compiler_params=params,
        cost_estimate=cost(2e9, 14 * MIB),
    )(halo, voltages, window, table, sign, late)
    got = lax.all_to_all(sent, ("feed", "tm"), split_axis=0, concat_axis=0, tiled=True)
    inputs = N_FEED * IN_DEV
    rows = LIVE_DEV * 256
    return pl.pallas_call(
        beam_kernel,
        name="beams_and_power",
        in_specs=[in_vmem] * 4,
        out_specs=in_vmem,
        out_shape=jax.ShapeDtypeStruct((LIVE_DEV, UPCH, CYL * NS), f32),
        scratch_shapes=[
            pltpu.VMEM((rows, inputs), bf16),
            pltpu.VMEM((2, NS, inputs), bf16),
            pltpu.VMEM((2 * CYL, rows // 2, 2 * NS), bf16),
            pltpu.VMEM((2 * CYL, rows // 2, 2 * NS), f32),
            pltpu.VMEM((2, rows, CYL * NS), bf16),
        ],
        compiler_params=pltpu.CompilerParams(vmem_limit_bytes=36 * MIB),
        cost_estimate=cost(9e9, 6 * MIB),
    )(
        got,
        feed_slot.reshape(1, inputs),
        jnp.asarray(position_table(), dtype=bf16),
        jnp.asarray(sub_channel_table(), dtype=bf16),
    )


def solution(mesh):
    in_specs = (P("feed", "tm"), P(), P())
    out_specs = P(("feed", "tm"), None, None)
    return jax.shard_map(local, mesh=mesh, in_specs=in_specs, out_specs=out_specs, check_vma=False)
```

```python
import math

import jax
import jax.numpy as jnp
import numpy as np
from jax import lax
from jax.experimental import pallas as pl
from jax.experimental.pallas import tpu as pltpu
from jax.sharding import PartitionSpec as P

CHANNELS = 1024
TAPS = 4
CYL = 4
NS = 256
UPCH = 16
FRAME = 2048
N_FEED = 32
N_TM = 8
IN_DEV = 64
FR_DEV = 16
LIVE_DEV = 3
LIVE = 768
OWNERS = 256
OWNER_BLOCK = 64
PAIRS = FR_DEV // 2
EARLY = 4
MIB = 1 << 20


def window_table():
    length = TAPS * FRAME
    sample = np.arange(length, dtype=np.float64)
    offset = (sample - length / 2 + 0.5) / FRAME
    taper = 0.5 - 0.5 * np.cos(2.0 * np.pi * (sample + 0.5) / length)
    return (np.sinc(offset) * taper).reshape(TAPS, FRAME).astype(np.float32)


def cos_sin(modulus, first, second):
    product = np.arange(first)[:, None] * np.arange(second)[None, :] % modulus
    angle = product * (2.0 * np.pi / modulus)
    scale = 1.0 / math.sqrt(modulus)
    return np.cos(angle) * scale, np.sin(angle) * scale


def position_table():
    cosine, sine = cos_sin(NS, NS, NS)
    return np.block([[cosine, -sine], [sine, cosine]])


def sub_channel_table():
    cosine, sine = cos_sin(UPCH, UPCH, UPCH)
    real = np.stack([cosine, sine])
    imag = np.stack([-sine, cosine])
    both = np.stack([real, imag]).reshape(2, 2, PAIRS, 2, UPCH)
    return np.einsum("qrghk,bd->qbkdhrg", both, np.eye(N_TM)).reshape(256, 256)


def unit_circle(phase):
    quadrant = (phase + 256) >> 9
    x = (phase - (quadrant << 9)).astype(jnp.float32) * np.float32(2.0 * np.pi / FRAME)
    x2 = x * x
    c = 1.0 + x2 * (-0.5 + x2 * (1.0 / 24 + x2 * (-1.0 / 720 + x2 * (1.0 / 40320))))
    s = x * (1.0 + x2 * (-1.0 / 6 + x2 * (1.0 / 120 + x2 * (-1.0 / 5040 + x2 * (1.0 / 362880)))))
    odd = (quadrant & 1) == 1
    cos_mag = jnp.where(odd, s, c)
    sin_mag = jnp.where(odd, c, s)
    cosine = jnp.where(((quadrant + 1) & 2) == 2, -cos_mag, cos_mag)
    sine = jnp.where((quadrant & 2) == 2, -sin_mag, sin_mag)
    return cosine, sine


def fold_frames(*args):
    odd = lax.axis_index("feed") & 1
    for swap in range(2):

        @pl.when(odd == swap)
        def _():
            fold_placed(swap, *args)


def fold_placed(swap, window_ref, load, frames, even_ref, odd_ref, middle_ref, last_ref):
    lane = lax.broadcasted_iota(jnp.int32, (16, 128), 1)
    back = (128 - lane) & 127
    last_ref[...] = jnp.zeros_like(last_ref)

    def piece(v, carry):
        sides = [pl.multiple_of(v * 128, 128), pl.multiple_of((FRAME // 128 - 1 - v) * 128, 128)]
        taps = [[window_ref[pl.ds(t, 1), pl.ds(side, 128)] for t in range(TAPS)] for side in sides]
        for rows in range(0, IN_DEV, 16):
            held = [{}, {}]
            for n, f in enumerate(frames):
                total = [None, None]
                for j in range(2):
                    for t in range(TAPS):
                        g = f - TAPS + 1 + t
                        if g not in held[j]:
                            held[j][g] = load(g, rows, sides[j]).astype(jnp.float32)
                        term = taps[j][t] * held[j][g]
                        total[j] = term if t == 0 else total[j] + term
                at = slice((n ^ swap) * IN_DEV + rows, (n ^ swap) * IN_DEV + rows + 16)
                turned = jnp.take_along_axis(total[1], back, axis=1, mode="promise_in_bounds")
                mirror = jnp.where(lane == 0, last_ref[at, :], turned)
                last_ref[at, :] = turned
                even_ref[at, pl.ds(sides[0], 128)] = (total[0] + mirror).astype(jnp.bfloat16)
                odd_ref[at, pl.ds(sides[0], 128)] = (total[0] - mirror).astype(jnp.bfloat16)
                middle_ref[at, :] = total[1].astype(jnp.bfloat16)
        return carry

    lax.fori_loop(0, FRAME // 256, piece, 0)


def table_kernel(flags_ref, table_ref, sign_ref, below_ref, channel_ref):
    lane = lax.broadcasted_iota(jnp.int32, (64, 128), 1)
    upto = (lax.broadcasted_iota(jnp.int32, (128, 128), 0) <= lax.broadcasted_iota(jnp.int32, (128, 128), 1)).astype(
        jnp.float32
    )
    ones = jnp.ones((128, 128), jnp.float32)
    sums = jnp.concatenate([upto, ones], axis=1).astype(jnp.bfloat16)
    ones = ones.astype(jnp.bfloat16)
    flags = flags_ref[...].astype(jnp.float32)
    flags = jnp.concatenate([flags, jnp.zeros_like(flags)], axis=0).astype(jnp.bfloat16)
    count = jnp.dot(flags, sums, preferred_element_type=jnp.float32)
    earlier = jnp.zeros((1, 128), jnp.float32)
    counts = []
    for r in range(CHANNELS // 128):
        counts.append((count[r : r + 1, :128] + earlier).astype(jnp.int32))
        earlier = earlier + count[r : r + 1, 128:]

    def ranks(step, carry):
        row = lax.broadcasted_iota(jnp.int32, (64, 128), 0) + step * 64
        rank = (row & (OWNERS - 1)) * LIVE_DEV + (row >> 8)
        at = pl.ds(pl.multiple_of(step * 64, 64), 64)
        below_ref[at, :] = sum((c <= rank).astype(jnp.float32) for c in counts).astype(jnp.bfloat16)
        return carry

    lax.fori_loop(0, LIVE // 64, ranks, 0)
    channel_ref[...] = jnp.dot(below_ref[...], ones, preferred_element_type=jnp.float32)

    def turn(step, carry):
        at = pl.ds(pl.multiple_of(step * 64, 64), 64)
        channel = channel_ref[at, :].astype(jnp.int32)
        scale = np.float32(1.0 / math.sqrt(FRAME))
        c, s = unit_circle((channel * lane) & (FRAME - 1))
        c, s = c * scale, s * scale
        dc, ds = unit_circle((channel * 128) & (FRAME - 1))
        sign = (1 - 2 * (channel & 1)).astype(jnp.float32) * scale
        sign_ref[at, :] = jnp.where(lane == 0, sign, 0.0).astype(jnp.bfloat16)
        for v in range(FRAME // 256):
            table_ref[0, at, v * 128 : (v + 1) * 128] = c.astype(jnp.bfloat16)
            table_ref[1, at, v * 128 : (v + 1) * 128] = (-s).astype(jnp.bfloat16)
            if v < FRAME // 256 - 1:
                c, s = dc * c - ds * s, ds * c + dc * s
        return carry

    lax.fori_loop(0, LIVE // 64, turn, 0)


def late_kernel(volt_ref, window_ref, _, even_ref, odd_ref, middle_ref, last_ref):
    def load(f, rows, lane):
        return volt_ref[rows : rows + 16, pl.ds(pl.multiple_of(f * FRAME + lane, 128), 128)]

    fold_frames(window_ref, load, range(EARLY, FR_DEV), even_ref, odd_ref, middle_ref, last_ref)


def transposed_dot(a, b):
    return lax.dot_general(a, b, (((1,), (1,)), ((), ())), preferred_element_type=jnp.float32)


def put_spectra(table_ref, sign_ref, even, odd, middle, wide_ref, first):
    real = transposed_dot(table_ref[0], even) + transposed_dot(sign_ref[...], middle)
    for r, value in enumerate((real, transposed_dot(table_ref[1], odd))):
        for c in range(LIVE_DEV):
            for h in range(2):
                part = value[c * OWNERS : (c + 1) * OWNERS, h * 128 : (h + 1) * 128]
                wide_ref[c, pl.ds(r * PAIRS + first + h, OWNERS, 2 * PAIRS), :] = part


def late_spectra_kernel(table_ref, sign_ref, even_ref, odd_ref, middle_ref, wide_ref):
    for n in range(PAIRS // 2 - 1):
        rows = slice(n * 256, (n + 1) * 256)
        put_spectra(table_ref, sign_ref, even_ref[rows, :], odd_ref[rows, :], middle_ref[rows, :], wide_ref, 2 * (n + 1))


def spectra_kernel(
    halo_ref, volt_ref, window_ref, table_ref, sign_ref, late_ref, out_ref, even_ref, odd_ref, middle_ref, last_ref, wide_ref
):
    step = pl.program_id(0)

    @pl.when(step == 0)
    def _():
        def load(f, rows, lane):
            ref, g = (halo_ref, f + TAPS - 1) if f < 0 else (volt_ref, f)
            return ref[rows : rows + 16, pl.ds(pl.multiple_of(g * FRAME + lane, 128), 128)]

        fold_frames(window_ref, load, range(EARLY), even_ref, odd_ref, middle_ref, last_ref)
        put_spectra(table_ref, sign_ref, even_ref[...], odd_ref[...], middle_ref[...], wide_ref, 0)

    size = OWNER_BLOCK * 2 * PAIRS
    early = lax.broadcasted_iota(jnp.int32, (size, 128), 0) & (PAIRS - 1) < EARLY // 2
    rows = pl.ds(pl.multiple_of(step * size, size), size)
    for c in range(LIVE_DEV):
        value = jnp.where(early, wide_ref[c, rows, :], late_ref[c, rows, :])
        part = slice(c * 2 * PAIRS, (c + 1) * 2 * PAIRS)
        out_ref[:, part, :] = value.reshape(OWNER_BLOCK, 2 * PAIRS, 128).astype(jnp.bfloat16)


def beam_kernel(recv_ref, slot_ref, position_ref, sub_ref, out_ref, x_ref, place_ref, cell_ref, part_ref, beam_ref):
    low = lax.broadcasted_iota(jnp.int32, (2 * PAIRS, 128), 1) < IN_DEV
    groups = 2 * CYL

    def pairs(s, carry):
        lane = pl.multiple_of(s * 128, 128)
        for c in range(LIVE_DEV):
            for b in range(N_TM):
                part = slice(c * 2 * PAIRS, (c + 1) * 2 * PAIRS)
                one = recv_ref[2 * s * N_TM + b, part]
                two = recv_ref[(2 * s + 1) * N_TM + b, part]
                even = jnp.where(low, one, two)
                odd = pltpu.roll(jnp.where(low, two, one).astype(jnp.float32), 64, 1)
                row = c * 256 + b * 32
                x_ref[row : row + 16, pl.ds(lane, 128)] = even
                x_ref[row + 16 : row + 32, pl.ds(lane, 128)] = odd.astype(jnp.bfloat16)
        return carry

    lax.fori_loop(0, N_FEED // 2, pairs, 0)
    slot = slot_ref[...]
    for i in range(groups):
        want = lax.broadcasted_iota(jnp.int32, (NS, N_FEED * IN_DEV), 0) + i * NS
        place_ref[i % 2] = (slot == want).astype(jnp.float32).astype(jnp.bfloat16)
        cells = transposed_dot(x_ref[...], place_ref[i % 2])
        cells = cells.reshape(-1, 2, PAIRS, NS)
        both = [cells[:, r].reshape(-1, NS) for r in range(2)]
        cell_ref[i] = jnp.concatenate(both, axis=1).astype(jnp.bfloat16)
    for p in range(2):
        for i in range(p * CYL, (p + 1) * CYL):
            part_ref[i] = jnp.dot(cell_ref[i], position_ref[...], preferred_element_type=jnp.float32)
        for f in range(LIVE_DEV * 16):
            rows = slice(f * PAIRS, (f + 1) * PAIRS)
            re = [part_ref[p * CYL + y, rows, :NS] for y in range(CYL)]
            im = [part_ref[p * CYL + y, rows, NS:] for y in range(CYL)]
            re_s, re_d = re[0] + re[2], re[0] - re[2]
            im_s, im_d = im[0] + im[2], im[0] - im[2]
            re_t, re_e = re[1] + re[3], re[1] - re[3]
            im_t, im_e = im[1] + im[3], im[1] - im[3]
            out_re = [re_s + re_t, re_d + im_e, re_s - re_t, re_d - im_e]
            out_im = [im_s + im_t, im_d - re_e, im_s - im_t, im_d + re_e]
            at = slice(f * 2 * PAIRS, (f + 1) * 2 * PAIRS)
            for e in range(CYL):
                value = jnp.concatenate([out_re[e], out_im[e]], axis=0) * 0.5
                beam_ref[p, at, e * NS : (e + 1) * NS] = value.astype(jnp.bfloat16)
    for c in range(LIVE_DEV):
        for e in range(CYL):
            total = None
            for p in range(2):
                beams = beam_ref[p, c * 256 : (c + 1) * 256, e * NS : (e + 1) * NS]
                up = jnp.dot(sub_ref[...], beams, preferred_element_type=jnp.float32)
                power = jnp.sum((up * up).reshape(2 * N_TM, UPCH, NS), axis=0)
                total = power if p == 0 else total + power
            out_ref[c, :, e * NS : (e + 1) * NS] = total * (1.0 / (2.0 * N_TM * (FR_DEV // UPCH)))


def cost(flops, nbytes):
    return pl.CostEstimate(flops=int(flops), bytes_accessed=int(nbytes), transcendentals=0)


def local(voltages, feed_slot, channel_flags):
    bf16, f32 = jnp.bfloat16, jnp.float32
    history = voltages[:, (FR_DEV - TAPS + 1) * FRAME :]
    halo = lax.ppermute(history, "tm", [(i, i + 1) for i in range(N_TM - 1)])
    window = jnp.asarray(window_table())
    in_vmem = pl.BlockSpec(memory_space=pltpu.VMEM)
    late_rows = (FR_DEV - EARLY) * IN_DEV
    early_rows = EARLY * IN_DEV
    params = pltpu.CompilerParams(vmem_limit_bytes=32 * MIB)
    half = FRAME // 2
    table, sign = pl.pallas_call(
        table_kernel,
        name="channel_table",
        out_shape=[jax.ShapeDtypeStruct((2, LIVE, half), bf16), jax.ShapeDtypeStruct((LIVE, 128), bf16)],
        scratch_shapes=[pltpu.VMEM((LIVE, 128), bf16), pltpu.VMEM((LIVE, 128), f32)],
        compiler_params=params,
        cost_estimate=cost(4e9, 3 * MIB),
    )(channel_flags.reshape(CHANNELS // 128, 128))
    folded = pl.pallas_call(
        late_kernel,
        name="filter",
        in_specs=[in_vmem, in_vmem, pl.BlockSpec(memory_space=pl.ANY)],
        out_shape=[
            jax.ShapeDtypeStruct((late_rows, half), bf16),
            jax.ShapeDtypeStruct((late_rows, half), bf16),
            jax.ShapeDtypeStruct((late_rows, 128), bf16),
        ],
        scratch_shapes=[pltpu.VMEM((late_rows, 128), f32)],
        compiler_params=params,
        cost_estimate=cost(4e9, 7 * MIB),
    )(voltages, window, table)
    late = pl.pallas_call(
        late_spectra_kernel,
        name="late_spectra",
        in_specs=[in_vmem] * 5,
        out_specs=in_vmem,
        out_shape=jax.ShapeDtypeStruct((LIVE_DEV, OWNERS * 2 * PAIRS, 128), f32),
        compiler_params=params,
        cost_estimate=cost(4e9, 12 * MIB),
    )(table, sign, *folded)
    sent = pl.pallas_call(
        spectra_kernel,
        name="spectra",
        grid=(OWNERS // OWNER_BLOCK,),
        in_specs=[in_vmem] * 6,
        out_specs=pl.BlockSpec((OWNER_BLOCK, LIVE_DEV * 2 * PAIRS, 128), lambda step: (step, 0, 0)),
        out_shape=pltpu.HBM((OWNERS, LIVE_DEV * 2 * PAIRS, 128), bf16),
        scratch_shapes=[
            pltpu.VMEM((early_rows, half), bf16),
            pltpu.VMEM((early_rows, half), bf16),
            pltpu.VMEM((early_rows, 128), bf16),
            pltpu.VMEM((early_rows, 128), f32),
            pltpu.VMEM((LIVE_DEV, OWNERS * 2 * PAIRS, 128), f32),
        ],
        compiler_params=params,
        cost_estimate=cost(2e9, 14 * MIB),
    )(halo, voltages, window, table, sign, late)
    got = lax.all_to_all(sent, ("feed", "tm"), split_axis=0, concat_axis=0, tiled=True)
    inputs = N_FEED * IN_DEV
    rows = LIVE_DEV * 256
    return pl.pallas_call(
        beam_kernel,
        name="beams_and_power",
        in_specs=[in_vmem] * 4,
        out_specs=in_vmem,
        out_shape=jax.ShapeDtypeStruct((LIVE_DEV, UPCH, CYL * NS), f32),
        scratch_shapes=[
            pltpu.VMEM((rows, inputs), bf16),
            pltpu.VMEM((2, NS, inputs), bf16),
            pltpu.VMEM((2 * CYL, rows // 2, 2 * NS), bf16),
            pltpu.VMEM((2 * CYL, rows // 2, 2 * NS), f32),
            pltpu.VMEM((2, rows, CYL * NS), bf16),
        ],
        compiler_params=pltpu.CompilerParams(vmem_limit_bytes=36 * MIB),
        cost_estimate=cost(9e9, 6 * MIB),
    )(
        got,
        feed_slot.reshape(1, inputs),
        jnp.asarray(position_table(), dtype=bf16),
        jnp.asarray(sub_channel_table(), dtype=bf16),
    )


def solution(mesh):
    in_specs = (P("feed", "tm"), P(), P())
    out_specs = P(("feed", "tm"), None, None)
    return jax.shard_map(local, mesh=mesh, in_specs=in_specs, out_specs=out_specs, check_vma=False)
```

```python
import math

import jax
import jax.numpy as jnp
import numpy as np
from jax import lax
from jax.experimental import pallas as pl
from jax.experimental.pallas import tpu as pltpu
from jax.sharding import PartitionSpec as P

CHANNELS = 1024
TAPS = 4
CYL = 4
NS = 256
UPCH = 16
FRAME = 2048
N_FEED = 32
N_TM = 8
IN_DEV = 64
FR_DEV = 16
LIVE_DEV = 3
LIVE = 768
OWNERS = 256
OWNER_BLOCK = 64
PAIRS = FR_DEV // 2
EARLY = 4
MIB = 1 << 20


def window_table():
    length = TAPS * FRAME
    sample = np.arange(length, dtype=np.float64)
    offset = (sample - length / 2 + 0.5) / FRAME
    taper = 0.5 - 0.5 * np.cos(2.0 * np.pi * (sample + 0.5) / length)
    return (np.sinc(offset) * taper).reshape(TAPS, FRAME).astype(np.float32)


def cos_sin(modulus, first, second):
    product = np.arange(first)[:, None] * np.arange(second)[None, :] % modulus
    angle = product * (2.0 * np.pi / modulus)
    scale = 1.0 / math.sqrt(modulus)
    return np.cos(angle) * scale, np.sin(angle) * scale


def position_table():
    cosine, sine = cos_sin(NS, NS, NS)
    return np.block([[cosine, -sine], [sine, cosine]])


def sub_channel_table():
    cosine, sine = cos_sin(UPCH, UPCH, UPCH)
    real = np.stack([cosine, sine])
    imag = np.stack([-sine, cosine])
    both = np.stack([real, imag]).reshape(2, 2, PAIRS, 2, UPCH)
    return np.einsum("qrghk,bd->qbkdhrg", both, np.eye(N_TM)).reshape(256, 256)


def unit_circle(phase):
    quadrant = (phase + 256) >> 9
    x = (phase - (quadrant << 9)).astype(jnp.float32) * np.float32(2.0 * np.pi / FRAME)
    x2 = x * x
    c = 1.0 + x2 * (-0.5 + x2 * (1.0 / 24 + x2 * (-1.0 / 720 + x2 * (1.0 / 40320))))
    s = x * (1.0 + x2 * (-1.0 / 6 + x2 * (1.0 / 120 + x2 * (-1.0 / 5040 + x2 * (1.0 / 362880)))))
    odd = (quadrant & 1) == 1
    cos_mag = jnp.where(odd, s, c)
    sin_mag = jnp.where(odd, c, s)
    cosine = jnp.where(((quadrant + 1) & 2) == 2, -cos_mag, cos_mag)
    sine = jnp.where((quadrant & 2) == 2, -sin_mag, sin_mag)
    return cosine, sine


def fold_frames(*args):
    odd = lax.axis_index("feed") & 1
    for swap in range(2):

        @pl.when(odd == swap)
        def _():
            fold_placed(swap, *args)


def fold_placed(swap, window_ref, load, frames, even_ref, odd_ref, middle_ref, last_ref):
    lane = lax.broadcasted_iota(jnp.int32, (16, 128), 1)
    back = (128 - lane) & 127
    last_ref[...] = jnp.zeros_like(last_ref)

    def piece(v, carry):
        sides = [pl.multiple_of(v * 128, 128), pl.multiple_of((FRAME // 128 - 1 - v) * 128, 128)]
        taps = [[window_ref[pl.ds(t, 1), pl.ds(side, 128)] for t in range(TAPS)] for side in sides]
        for rows in range(0, IN_DEV, 16):
            held = [{}, {}]
            for n, f in enumerate(frames):
                total = [None, None]
                for j in range(2):
                    for t in range(TAPS):
                        g = f - TAPS + 1 + t
                        if g not in held[j]:
                            held[j][g] = load(g, rows, sides[j]).astype(jnp.float32)
                        term = taps[j][t] * held[j][g]
                        total[j] = term if t == 0 else total[j] + term
                at = slice((n ^ swap) * IN_DEV + rows, (n ^ swap) * IN_DEV + rows + 16)
                turned = jnp.take_along_axis(total[1], back, axis=1, mode="promise_in_bounds")
                mirror = jnp.where(lane == 0, last_ref[at, :], turned)
                last_ref[at, :] = turned
                even_ref[at, pl.ds(sides[0], 128)] = (total[0] + mirror).astype(jnp.bfloat16)
                odd_ref[at, pl.ds(sides[0], 128)] = (total[0] - mirror).astype(jnp.bfloat16)
                middle_ref[at, :] = total[1].astype(jnp.bfloat16)
        return carry

    lax.fori_loop(0, FRAME // 256, piece, 0)


def table_kernel(flags_ref, table_ref, sign_ref, below_ref, channel_ref):
    lane = lax.broadcasted_iota(jnp.int32, (64, 128), 1)
    upto = (lax.broadcasted_iota(jnp.int32, (128, 128), 0) <= lax.broadcasted_iota(jnp.int32, (128, 128), 1)).astype(
        jnp.float32
    )
    ones = jnp.ones((128, 128), jnp.float32)
    sums = jnp.concatenate([upto, ones], axis=1).astype(jnp.bfloat16)
    ones = ones.astype(jnp.bfloat16)
    flags = flags_ref[...].astype(jnp.float32)
    flags = jnp.concatenate([flags, jnp.zeros_like(flags)], axis=0).astype(jnp.bfloat16)
    count = jnp.dot(flags, sums, preferred_element_type=jnp.float32)
    earlier = jnp.zeros((1, 128), jnp.float32)
    counts = []
    for r in range(CHANNELS // 128):
        counts.append((count[r : r + 1, :128] + earlier).astype(jnp.int32))
        earlier = earlier + count[r : r + 1, 128:]

    def ranks(step, carry):
        row = lax.broadcasted_iota(jnp.int32, (64, 128), 0) + step * 64
        rank = (row & (OWNERS - 1)) * LIVE_DEV + (row >> 8)
        at = pl.ds(pl.multiple_of(step * 64, 64), 64)
        below_ref[at, :] = sum((c <= rank).astype(jnp.float32) for c in counts).astype(jnp.bfloat16)
        return carry

    lax.fori_loop(0, LIVE // 64, ranks, 0)
    channel_ref[...] = jnp.dot(below_ref[...], ones, preferred_element_type=jnp.float32)

    def turn(step, carry):
        at = pl.ds(pl.multiple_of(step * 64, 64), 64)
        channel = channel_ref[at, :].astype(jnp.int32)
        scale = np.float32(1.0 / math.sqrt(FRAME))
        c, s = unit_circle((channel * lane) & (FRAME - 1))
        c, s = c * scale, s * scale
        dc, ds = unit_circle((channel * 128) & (FRAME - 1))
        sign = (1 - 2 * (channel & 1)).astype(jnp.float32) * scale
        sign_ref[at, :] = jnp.where(lane == 0, sign, 0.0).astype(jnp.bfloat16)
        for v in range(FRAME // 256):
            table_ref[0, at, v * 128 : (v + 1) * 128] = c.astype(jnp.bfloat16)
            table_ref[1, at, v * 128 : (v + 1) * 128] = (-s).astype(jnp.bfloat16)
            if v < FRAME // 256 - 1:
                c, s = dc * c - ds * s, ds * c + dc * s
        return carry

    lax.fori_loop(0, LIVE // 64, turn, 0)


def late_kernel(volt_ref, window_ref, _, even_ref, odd_ref, middle_ref, last_ref):
    def load(f, rows, lane):
        return volt_ref[rows : rows + 16, pl.ds(pl.multiple_of(f * FRAME + lane, 128), 128)]

    fold_frames(window_ref, load, range(EARLY, FR_DEV), even_ref, odd_ref, middle_ref, last_ref)


def transposed_dot(a, b):
    return lax.dot_general(a, b, (((1,), (1,)), ((), ())), preferred_element_type=jnp.float32)


def put_spectra(table_ref, sign_ref, even, odd, middle, wide_ref, first):
    real = transposed_dot(table_ref[0], even) + transposed_dot(sign_ref[...], middle)
    for r, value in enumerate((real, transposed_dot(table_ref[1], odd))):
        for c in range(LIVE_DEV):
            for h in range(2):
                part = value[c * OWNERS : (c + 1) * OWNERS, h * 128 : (h + 1) * 128]
                wide_ref[c, pl.ds(r * PAIRS + first + h, OWNERS, 2 * PAIRS), :] = part


def late_spectra_kernel(table_ref, sign_ref, even_ref, odd_ref, middle_ref, wide_ref):
    for n in range(PAIRS // 2 - 1):
        rows = slice(n * 256, (n + 1) * 256)
        put_spectra(table_ref, sign_ref, even_ref[rows, :], odd_ref[rows, :], middle_ref[rows, :], wide_ref, 2 * (n + 1))


def spectra_kernel(
    halo_ref, volt_ref, window_ref, table_ref, sign_ref, late_ref, out_ref, even_ref, odd_ref, middle_ref, last_ref, wide_ref
):
    step = pl.program_id(0)

    @pl.when(step == 0)
    def _():
        def load(f, rows, lane):
            ref, g = (halo_ref, f + TAPS - 1) if f < 0 else (volt_ref, f)
            return ref[rows : rows + 16, pl.ds(pl.multiple_of(g * FRAME + lane, 128), 128)]

        fold_frames(window_ref, load, range(EARLY), even_ref, odd_ref, middle_ref, last_ref)
        put_spectra(table_ref, sign_ref, even_ref[...], odd_ref[...], middle_ref[...], wide_ref, 0)

    size = OWNER_BLOCK * 2 * PAIRS
    early = lax.broadcasted_iota(jnp.int32, (size, 128), 0) & (PAIRS - 1) < EARLY // 2
    rows = pl.ds(pl.multiple_of(step * size, size), size)
    for c in range(LIVE_DEV):
        value = jnp.where(early, wide_ref[c, rows, :], late_ref[c, rows, :])
        part = slice(c * 2 * PAIRS, (c + 1) * 2 * PAIRS)
        out_ref[:, part, :] = value.reshape(OWNER_BLOCK, 2 * PAIRS, 128).astype(jnp.bfloat16)


def beam_kernel(recv_ref, slot_ref, position_ref, sub_ref, out_ref, x_ref, place_ref, cell_ref, part_ref, beam_ref):
    low = lax.broadcasted_iota(jnp.int32, (2 * PAIRS, 128), 1) < IN_DEV
    groups = 2 * CYL

    def pairs(s, carry):
        lane = pl.multiple_of(s * 128, 128)
        for c in range(LIVE_DEV):
            for b in range(N_TM):
                part = slice(c * 2 * PAIRS, (c + 1) * 2 * PAIRS)
                one = recv_ref[2 * s * N_TM + b, part]
                two = recv_ref[(2 * s + 1) * N_TM + b, part]
                even = jnp.where(low, one, two)
                odd = pltpu.roll(jnp.where(low, two, one), 64, 1)
                row = c * 256 + b * 32
                x_ref[row : row + 16, pl.ds(lane, 128)] = even
                x_ref[row + 16 : row + 32, pl.ds(lane, 128)] = odd
        return carry

    lax.fori_loop(0, N_FEED // 2, pairs, 0)
    slot = slot_ref[...]
    for i in range(groups):
        want = lax.broadcasted_iota(jnp.int32, (NS, N_FEED * IN_DEV), 0) + i * NS
        place_ref[i % 2] = (slot == want).astype(jnp.float32).astype(jnp.bfloat16)
        cells = transposed_dot(x_ref[...], place_ref[i % 2])
        cells = cells.reshape(-1, 2, PAIRS, NS)
        both = [cells[:, r].reshape(-1, NS) for r in range(2)]
        cell_ref[i] = jnp.concatenate(both, axis=1).astype(jnp.bfloat16)
    for p in range(2):
        for i in range(p * CYL, (p + 1) * CYL):
            part_ref[i] = jnp.dot(cell_ref[i], position_ref[...], preferred_element_type=jnp.float32)
        for f in range(LIVE_DEV * 16):
            rows = slice(f * PAIRS, (f + 1) * PAIRS)
            re = [part_ref[p * CYL + y, rows, :NS] for y in range(CYL)]
            im = [part_ref[p * CYL + y, rows, NS:] for y in range(CYL)]
            re_s, re_d = re[0] + re[2], re[0] - re[2]
            im_s, im_d = im[0] + im[2], im[0] - im[2]
            re_t, re_e = re[1] + re[3], re[1] - re[3]
            im_t, im_e = im[1] + im[3], im[1] - im[3]
            out_re = [re_s + re_t, re_d + im_e, re_s - re_t, re_d - im_e]
            out_im = [im_s + im_t, im_d - re_e, im_s - im_t, im_d + re_e]
            at = slice(f * 2 * PAIRS, (f + 1) * 2 * PAIRS)
            for e in range(CYL):
                value = jnp.concatenate([out_re[e], out_im[e]], axis=0) * 0.5
                beam_ref[p, at, e * NS : (e + 1) * NS] = value.astype(jnp.bfloat16)
    for c in range(LIVE_DEV):
        for e in range(CYL):
            total = None
            for p in range(2):
                beams = beam_ref[p, c * 256 : (c + 1) * 256, e * NS : (e + 1) * NS]
                up = jnp.dot(sub_ref[...], beams, preferred_element_type=jnp.float32)
                power = jnp.sum((up * up).reshape(2 * N_TM, UPCH, NS), axis=0)
                total = power if p == 0 else total + power
            out_ref[c, :, e * NS : (e + 1) * NS] = total * (1.0 / (2.0 * N_TM * (FR_DEV // UPCH)))


def cost(flops, nbytes):
    return pl.CostEstimate(flops=int(flops), bytes_accessed=int(nbytes), transcendentals=0)


def local(voltages, feed_slot, channel_flags):
    bf16, f32 = jnp.bfloat16, jnp.float32
    history = voltages[:, (FR_DEV - TAPS + 1) * FRAME :]
    halo = lax.ppermute(history, "tm", [(i, i + 1) for i in range(N_TM - 1)])
    window = jnp.asarray(window_table())
    in_vmem = pl.BlockSpec(memory_space=pltpu.VMEM)
    late_rows = (FR_DEV - EARLY) * IN_DEV
    early_rows = EARLY * IN_DEV
    params = pltpu.CompilerParams(vmem_limit_bytes=32 * MIB)
    half = FRAME // 2
    table, sign = pl.pallas_call(
        table_kernel,
        name="channel_table",
        out_shape=[jax.ShapeDtypeStruct((2, LIVE, half), bf16), jax.ShapeDtypeStruct((LIVE, 128), bf16)],
        scratch_shapes=[pltpu.VMEM((LIVE, 128), bf16), pltpu.VMEM((LIVE, 128), f32)],
        compiler_params=params,
        cost_estimate=cost(4e9, 3 * MIB),
    )(channel_flags.reshape(CHANNELS // 128, 128))
    folded = pl.pallas_call(
        late_kernel,
        name="filter",
        in_specs=[in_vmem, in_vmem, pl.BlockSpec(memory_space=pl.ANY)],
        out_shape=[
            jax.ShapeDtypeStruct((late_rows, half), bf16),
            jax.ShapeDtypeStruct((late_rows, half), bf16),
            jax.ShapeDtypeStruct((late_rows, 128), bf16),
        ],
        scratch_shapes=[pltpu.VMEM((late_rows, 128), f32)],
        compiler_params=params,
        cost_estimate=cost(4e9, 7 * MIB),
    )(voltages, window, table)
    late = pl.pallas_call(
        late_spectra_kernel,
        name="late_spectra",
        in_specs=[in_vmem] * 5,
        out_specs=in_vmem,
        out_shape=jax.ShapeDtypeStruct((LIVE_DEV, OWNERS * 2 * PAIRS, 128), f32),
        compiler_params=params,
        cost_estimate=cost(4e9, 12 * MIB),
    )(table, sign, *folded)
    sent = pl.pallas_call(
        spectra_kernel,
        name="spectra",
        grid=(OWNERS // OWNER_BLOCK,),
        in_specs=[in_vmem] * 6,
        out_specs=pl.BlockSpec((OWNER_BLOCK, LIVE_DEV * 2 * PAIRS, 128), lambda step: (step, 0, 0)),
        out_shape=pltpu.HBM((OWNERS, LIVE_DEV * 2 * PAIRS, 128), bf16),
        scratch_shapes=[
            pltpu.VMEM((early_rows, half), bf16),
            pltpu.VMEM((early_rows, half), bf16),
            pltpu.VMEM((early_rows, 128), bf16),
            pltpu.VMEM((early_rows, 128), f32),
            pltpu.VMEM((LIVE_DEV, OWNERS * 2 * PAIRS, 128), f32),
        ],
        compiler_params=params,
        cost_estimate=cost(2e9, 14 * MIB),
    )(halo, voltages, window, table, sign, late)
    got = lax.all_to_all(sent, ("feed", "tm"), split_axis=0, concat_axis=0, tiled=True)
    inputs = N_FEED * IN_DEV
    rows = LIVE_DEV * 256
    return pl.pallas_call(
        beam_kernel,
        name="beams_and_power",
        in_specs=[in_vmem] * 4,
        out_specs=in_vmem,
        out_shape=jax.ShapeDtypeStruct((LIVE_DEV, UPCH, CYL * NS), f32),
        scratch_shapes=[
            pltpu.VMEM((rows, inputs), bf16),
            pltpu.VMEM((2, NS, inputs), bf16),
            pltpu.VMEM((2 * CYL, rows // 2, 2 * NS), bf16),
            pltpu.VMEM((2 * CYL, rows // 2, 2 * NS), f32),
            pltpu.VMEM((2, rows, CYL * NS), bf16),
        ],
        compiler_params=pltpu.CompilerParams(vmem_limit_bytes=36 * MIB),
        cost_estimate=cost(9e9, 6 * MIB),
    )(
        got,
        feed_slot.reshape(1, inputs),
        jnp.asarray(position_table(), dtype=bf16),
        jnp.asarray(sub_channel_table(), dtype=bf16),
    )


def solution(mesh):
    in_specs = (P("feed", "tm"), P(), P())
    out_specs = P(("feed", "tm"), None, None)
    return jax.shard_map(local, mesh=mesh, in_specs=in_specs, out_specs=out_specs, check_vma=False)
```
